32 devices in a mesh: group: 2 (over x), dp: 16 (over z, y, core).
Axes of the slice: x: 2, y: 2, z: 4, core: 2. Of those that a mesh axis runs over, the one named last changes fastest.
Arguments:
- tokens: bfloat16 [1024, 8192], P(('group', 'dp')), parts along dimension 0, may hold values from -6 to 6
- cotangent: bfloat16 [1024, 8192], P(('group', 'dp')), parts along dimension 0, may hold values from -6 to 6
- lengths: int32 [16], P('group'), parts along dimension 0, may hold values from 16 to 64, as said below
- gate_weight: bfloat16 [8192, 28672], P(None, 'dp'), may hold values from -0.0625 to 0.0625
- up_weight: bfloat16 [8192, 28672], P(None, 'dp'), may hold values from -0.0625 to 0.0625
- down_weight: bfloat16 [28672, 8192], P('dp'), may hold values from -0.0625 to 0.0625
- proj_input: bfloat16 [8192, 64], replicated, may hold values from -0.0625 to 0.0625
- proj_cotangent: bfloat16 [8192, 64], replicated, may hold values from -0.0625 to 0.0625
- proj_hidden: bfloat16 [28672, 64], P('dp'), may hold values from -0.03125 to 0.03125
- proj_up: bfloat16 [28672, 64], P('dp'), may hold values from -0.03125 to 0.03125
- proj_gate: bfloat16 [28672, 64], P('dp'), may hold values from -0.03125 to 0.03125
- queries: float32 [32, 12288], P('group', 'dp'), parts along dimension 0, may hold values from -0.0546875 to 0.0546875
Outputs:
- logged: float32 [16, 12288], P('group', 'dp'), parts along dimension 0
- scores: float32 [32, 8], P('group'), parts along dimension 0
The draws below stay inside these ranges and needn't reach their ends.
There are 2 independent parts, one for each index of `group`. The reference program is written for one: setup_inputs(seed, part) draws one part's arguments, and reference() takes and returns one part's arrays. A program takes and returns all parts, laid end to end along the dimension named above; an argument that names none is the same for every part. Nothing has to cross between parts.
Inputs may be any that keep to these rules, and one draw needn't show every extreme that they name: `lengths`: some sequence has exactly 64 live tokens and some exactly 16.
All inputs are finite; a program needn't handle non-finite values.
Results may differ from the reference program's by a relative error of at most 0.0031.
Values may be sent and summed in bfloat16 or wider, within the bound.
No kernel may reach another device: no remote copies, remote signals or barrier semaphores. Data moves between devices by JAX's collectives and lax.ppermute only.
A program may use at most 256 MiB of HBM per device.

```python
import math
import jax
import jax.numpy as jnp
from jax import lax

D = 8192
FF = 28672
RANK = 64
LEN = 64
SEQS = 8
NQ = 16
TOKENS = 512
SKETCH = 12288


def draw_lengths(key, part):
    key = jax.random.fold_in(key, 7)
    first_key, second_key = jax.random.split(key)
    values = jax.random.randint(first_key, (SEQS,), LEN // 4, LEN + 1)
    order = jax.random.permutation(second_key, SEQS)
    values = values.at[order[0]].set(LEN)
    values = values.at[order[1]].set(LEN // 4)
    return values.astype(jnp.int32)


def level_of(rng, extent, cuts, smallest, top_value):
    def one(position, parts):
        heights = jax.random.uniform(jax.random.fold_in(jax.random.fold_in(rng, 6), position), (parts,), jnp.float32, smallest / len(cuts), top_value / len(cuts))
        return jnp.repeat(jnp.exp(heights), extent[position] // parts).reshape((-1,) + (1,) * (len(extent) - position - 1))

    level = one(*cuts[0])
    for cut in cuts[1:]:
        level = level * one(*cut)
    return level


def centred(own_key, dims, width, most, cuts=(), kind=jnp.bfloat16):
    gain = level_of(own_key, dims, cuts, -0.22, 0.18) if cuts else 1.0
    result = jax.random.normal(own_key, dims, jnp.float32) * width * gain
    return jnp.minimum(jnp.maximum(result, -most), most).astype(kind)


def setup_inputs(seed: int = 0, part: int = 0) -> dict:
    keys = jax.random.split(jax.random.key(seed), 13)
    part_keys = jax.random.split(jax.random.fold_in(keys[12], part), 13)
    return {
        "tokens": centred(part_keys[0], (TOKENS, D), 1.0, 6.0, ((0, 16),)),
        "cotangent": centred(part_keys[1], (TOKENS, D), 1.0, 6.0, ((0, 16),)),
        "lengths": draw_lengths(jax.random.fold_in(jax.random.fold_in(keys[12], part), 71), part),
        "gate_weight": centred(keys[3], (D, FF), D ** -0.5, 0.0625, ((1, 16),)),
        "up_weight": centred(keys[4], (D, FF), D ** -0.5, 0.0625, ((1, 16),)),
        "down_weight": centred(keys[5], (FF, D), D ** -0.5, 0.0625, ((0, 16),)),
        "proj_input": centred(keys[6], (D, RANK), D ** -0.5, 0.0625),
        "proj_cotangent": centred(keys[7], (D, RANK), D ** -0.5, 0.0625),
        "proj_hidden": centred(keys[8], (FF, RANK), FF ** -0.5, 0.03125, ((0, 16),)),
        "proj_up": centred(keys[9], (FF, RANK), FF ** -0.5, 0.03125, ((0, 16),)),
        "proj_gate": centred(keys[10], (FF, RANK), FF ** -0.5, 0.03125, ((0, 16),)),
        "queries": centred(part_keys[11], (NQ, SKETCH), SKETCH ** -0.5, 0.0546875, ((1, 16),), jnp.float32),
    }


def sketch_of(weight_rows, out_proj, in_proj):
    out_blocks = out_proj.reshape(SEQS, LEN, RANK)
    in_blocks = in_proj.reshape(SEQS, LEN, RANK)
    sketch = jnp.einsum('sl,slo,sli->soi', weight_rows, out_blocks, in_blocks, precision=lax.Precision.HIGHEST)
    return sketch.reshape(SEQS, RANK * RANK)

def reference(tokens, cotangent, lengths, gate_weight, up_weight, down_weight, proj_input, proj_cotangent, proj_hidden, proj_up, proj_gate, queries):
    live = (jnp.arange(LEN, dtype=jnp.int32)[None, :] < lengths[:, None]).astype(jnp.float32)
    weight_rows = live * (1.0 / math.sqrt(LEN))
    gate = jnp.dot(tokens.astype(jnp.float32), gate_weight.astype(jnp.float32), preferred_element_type=jnp.float32)
    up = jnp.dot(tokens.astype(jnp.float32), up_weight.astype(jnp.float32), preferred_element_type=jnp.float32)
    sigma = jax.nn.sigmoid(gate)
    silu_val = gate * sigma
    silu_grad = sigma * (1.0 + gate * (1.0 - sigma))
    hidden = (silu_val * up).astype(jnp.bfloat16)
    dhidden = jnp.dot(cotangent.astype(jnp.float32), down_weight.T.astype(jnp.float32), preferred_element_type=jnp.float32)
    d_up = (dhidden * silu_val).astype(jnp.bfloat16)
    d_gate = (dhidden * up * silu_grad).astype(jnp.bfloat16)
    a_in = jnp.dot(tokens.astype(jnp.float32), proj_input.astype(jnp.float32), preferred_element_type=jnp.float32)
    a_cot = jnp.dot(cotangent.astype(jnp.float32), proj_cotangent.astype(jnp.float32), preferred_element_type=jnp.float32)
    a_hid = jnp.dot(hidden.astype(jnp.float32), proj_hidden.astype(jnp.float32), preferred_element_type=jnp.float32)
    a_up = jnp.dot(d_up.astype(jnp.float32), proj_up.astype(jnp.float32), preferred_element_type=jnp.float32)
    a_gate = jnp.dot(d_gate.astype(jnp.float32), proj_gate.astype(jnp.float32), preferred_element_type=jnp.float32)
    logged = jnp.concatenate([sketch_of(weight_rows, a_gate, a_in), sketch_of(weight_rows, a_up, a_in), sketch_of(weight_rows, a_cot, a_hid)], axis=1)
    gram = jnp.dot(logged, logged.T, precision=lax.Precision.HIGHEST)
    cross = jnp.dot(queries, logged.T, precision=lax.Precision.HIGHEST)
    damping = jnp.trace(gram) / SEQS
    system = gram + damping * jnp.eye(SEQS, dtype=jnp.float32)
    scores = damping * jnp.linalg.solve(system, cross.T).T
    return (logged, scores)
```

```python
import math

import jax
import jax.numpy as jnp
from jax import lax
from jax.experimental import pallas as pl
from jax.experimental.pallas import tpu as pltpu
from jax.sharding import PartitionSpec as P

RANK = 64
LEN = 64
SEQS = 8
HIGHEST = lax.Precision.HIGHEST
F32 = jnp.float32
BF16 = jnp.bfloat16


def silu_parts(gate):
    sigma = jax.nn.sigmoid(gate)
    return (gate * sigma, sigma * (1.0 + gate * (1.0 - sigma)))


def block_sketch(weight_rows, out_proj, in_proj):
    out_blocks = out_proj.reshape(SEQS, LEN, RANK)
    in_blocks = in_proj.reshape(SEQS, LEN, RANK)
    sketch = jnp.einsum(
        "sl,slo,sli->soi", weight_rows, out_blocks, in_blocks, precision=HIGHEST
    )
    return sketch.reshape(SEQS, RANK * RANK)


def on_device(
    tokens,
    cotangent,
    lengths,
    gate_weight,
    up_weight,
    down_weight,
    proj_input,
    proj_cotangent,
    proj_hidden,
    proj_up,
    proj_gate,
    queries,
):
    scale = 1.0 / math.sqrt(LEN)
    piece = lax.all_gather(tokens, "dp", axis=0, tiled=True)
    gate = jnp.dot(piece, gate_weight, preferred_element_type=F32)
    up = jnp.dot(piece, up_weight, preferred_element_type=F32)
    input_all = jnp.dot(piece, proj_input, preferred_element_type=F32)
    silu_val, silu_grad = silu_parts(gate)
    hidden = (silu_val * up).astype(BF16)
    piece = lax.all_gather(cotangent, "dp", axis=0, tiled=True)
    dhidden = lax.dot_general(
        piece, down_weight, (((1,), (1,)), ((), ())), preferred_element_type=F32
    )
    cot_all = jnp.dot(piece, proj_cotangent, preferred_element_type=F32)
    d_up = (dhidden * silu_val).astype(BF16)
    d_gate = (dhidden * up * silu_grad).astype(BF16)
    p_hid = jnp.dot(hidden, proj_hidden, preferred_element_type=F32)
    p_up = jnp.dot(d_up, proj_up, preferred_element_type=F32)
    p_gate = jnp.dot(d_gate, proj_gate, preferred_element_type=F32)
    a_hid, a_up, a_gate = lax.psum((p_hid, p_up, p_gate), "dp")
    live = (lax.iota(jnp.int32, LEN)[None, :] < lengths[:, None]).astype(F32) * scale
    logged = jnp.concatenate(
        [
            block_sketch(live, a_gate, input_all),
            block_sketch(live, a_up, input_all),
            block_sketch(live, cot_all, a_hid),
        ],
        axis=1,
    )
    width = queries.shape[1]
    logged_part = lax.dynamic_slice_in_dim(logged, lax.axis_index("dp") * width, width, 1)
    full_queries = lax.all_gather(queries, "dp", axis=1, tiled=True)
    gram = jnp.dot(logged, logged.T, precision=HIGHEST)
    cross = jnp.dot(full_queries, logged.T, precision=HIGHEST)
    damping = jnp.trace(gram) / SEQS
    system = gram + damping * jnp.eye(SEQS, dtype=F32)
    factor = jnp.linalg.cholesky(system)
    solved = jax.scipy.linalg.cho_solve((factor, True), cross.T)
    scores = damping * solved.T
    return (logged_part, scores)


PLACES = [(z, y, c) for z in range(4) for y in range(2) for c in range(2)]


def spot(z, y, c):
    return 4 * z + 2 * y + c


CORE = [(spot(z, y, c), spot(z, y, 1 - c)) for z, y, c in PLACES]
YSWAP = [(spot(z, y, c), spot(z, 1 - y, c)) for z, y, c in PLACES]
ZPAIR = [(spot(z, y, c), spot(z ^ 1, y, c)) for z, y, c in PLACES]
ZMID = [(spot(z, y, c), spot(3 - z, y, c)) for z, y, c in PLACES if z in (1, 2)]
ZOUT = [(spot(z, y, c), spot(z ^ 1, y, c)) for z, y, c in PLACES if z in (1, 2)]


def send(x, pairs):
    return lax.ppermute(x, "dp", pairs)


def send_z(x, targets):
    return send(x, [(spot(z, y, c), spot(targets[z], y, c)) for z, y, c in PLACES if z in targets])


def gather_near(x):
    half = x.shape[1] // 2
    from_z = send(x, ZPAIR)
    from_y = send(x, YSWAP)
    diag_z = send(from_y[:, :half], ZPAIR)
    diag_y = send(from_z[:, half:], YSWAP)
    diag = jnp.concatenate([diag_z, diag_y], axis=1)
    mine = jnp.concatenate([x, from_z, from_y, diag], axis=0)
    return mine, send(mine, CORE)


def gather_far(mine, z, y, parts):
    half = mine.shape[1] // 2
    step = half // parts
    rows = mine.shape[0] // 2
    turned = jnp.concatenate([mine[rows:, half:], mine[:rows, half:]], axis=0)
    share = jnp.where(y == 0, mine[:, :half], turned)
    pieces = []
    for part in range(parts):
        block = share[:, part * step : (part + 1) * step]
        middle = send(block, ZMID)
        outer = send(middle, ZOUT)
        got = jnp.where((z == 1) | (z == 2), middle, outer)
        other = send(got, YSWAP)
        low = jnp.where(y == 0, got, other)
        high = jnp.where(y == 0, other, got)
        both = jnp.concatenate([low, high], axis=1)
        both = jnp.concatenate([both, send(both, CORE)], axis=0)
        pieces.append(((part * step, step), both[:, :step]))
        pieces.append(((half + part * step, step), both[:, step:]))
    return pieces


def canonical(near, far, z, y, c):
    n = near.shape[1]
    near = near.reshape(2, 2, 2, 32, n)
    far = far.reshape(2, 2, 2, 32, n)
    near = jnp.where(z % 2 == 1, near[:, :, ::-1], near)
    near = jnp.where(y == 1, near[:, ::-1], near)
    far = jnp.where(z // 2 == 1, far[:, :, ::-1], far)
    both = jnp.stack([near, far])
    both = jnp.where(z // 2 == 1, both[::-1], both)
    both = jnp.where(c == 1, both[:, ::-1], both)
    both = both.transpose(0, 3, 2, 1, 4, 5)
    return both.reshape(512, n)


def dot_pieces(pieces, weight, axis):
    total = None
    for (start, size), block in pieces:
        part = lax.dot_general(
            block,
            lax.slice_in_dim(weight, start, start + size, axis=axis),
            (((1,), (axis,)), ((), ())),
            preferred_element_type=F32,
        )
        total = part if total is None else total + part
    return total


def dot(a, b):
    return jnp.dot(a, b, preferred_element_type=F32)


def sum_all(x):
    x = x + send(x, CORE)
    x = x + send(x, YSWAP)
    parts = [send_z(x, {z: (z + d) % 4 for z in range(4)}) for d in (1, 2, 3)]
    return (x + parts[1]) + (parts[0] + parts[2])


def solve_kernel(stats_ref, out_ref):
    stats = stats_ref[...]
    gram = stats[:SEQS]
    row = lax.broadcasted_iota(jnp.int32, (SEQS, SEQS), 0)
    col = lax.broadcasted_iota(jnp.int32, (SEQS, SEQS), 1)
    eye = (row == col).astype(F32)
    damping = jnp.sum(gram * eye) / SEQS
    left = gram + damping * eye
    right = eye
    for k in range(SEQS):
        pivot = left[k : k + 1, k : k + 1]
        left_row = left[k : k + 1, :] / pivot
        right_row = right[k : k + 1, :] / pivot
        factor = jnp.where(row[:, :1] == k, 0.0, left[:, k : k + 1])
        left = jnp.where(row == k, left_row, left - factor * left_row)
        right = jnp.where(row == k, right_row, right - factor * right_row)
    cross = stats[SEQS:]
    out_ref[...] = damping * jnp.dot(cross, right, precision=HIGHEST, preferred_element_type=F32)


def on_device_424(
    tokens,
    cotangent,
    lengths,
    gate_weight,
    up_weight,
    down_weight,
    proj_input,
    proj_cotangent,
    proj_hidden,
    proj_up,
    proj_gate,
    queries,
):
    index = lax.axis_index("dp")
    z, y, c = index // 4, (index // 2) % 2, index % 2
    far_parts = 2

    tok_mine, tok_other = gather_near(tokens)
    cot_mine, cot_other = gather_near(cotangent)
    tok_far = gather_far(tok_mine, z, y, far_parts)
    cot_far = gather_far(cot_mine, z, y, far_parts)

    tok_near = jnp.concatenate([tok_mine, tok_other], axis=0)
    gate_near = dot(tok_near, gate_weight)
    up_near = dot(tok_near, up_weight)
    cot_near = jnp.concatenate([cot_mine, cot_other], axis=0)
    dh_near = lax.dot_general(
        cot_near, down_weight, (((1,), (1,)), ((), ())), preferred_element_type=F32
    )
    gate_far = dot_pieces(tok_far, gate_weight, 0)
    up_far = dot_pieces(tok_far, up_weight, 0)
    dh_far = dot_pieces(cot_far, down_weight, 1)

    def layer(gate, up, dhidden):
        silu_val, silu_grad = silu_parts(gate)
        hidden = (silu_val * up).astype(BF16)
        d_up = (dhidden * silu_val).astype(BF16)
        d_gate = (dhidden * up * silu_grad).astype(BF16)
        return dot(hidden, proj_hidden), dot(d_gate, proj_gate), dot(d_up, proj_up)

    hid_near, pg_near, pu_near = layer(gate_near, up_near, dh_near)
    hid_far, pg_far, pu_far = layer(gate_far, up_far, dh_far)

    a_in = canonical(dot(tok_near, proj_input), dot_pieces(tok_far, proj_input, 0), z, y, c)
    a_cot = canonical(dot(cot_near, proj_cotangent), dot_pieces(cot_far, proj_cotangent, 0), z, y, c)
    a_hid = sum_all(canonical(hid_near, hid_far, z, y, c))

    p_near = jnp.concatenate([pg_near, pu_near], axis=1)
    p_far = jnp.concatenate([pg_far, pu_far], axis=1)
    p = canonical(p_near, p_far, z, y, c).T
    mine = 3 * RANK // 16
    slots = -(-2 * RANK // mine)
    slots = -(-slots // 4) * 4
    p = jnp.pad(p, ((0, slots * mine - 2 * RANK), (0, 0))).reshape(slots // 4, 2, 2, mine, -1)
    keep = jnp.where(c == 0, p[:, :, 0], p[:, :, 1])
    give = jnp.where(c == 0, p[:, :, 1], p[:, :, 0])
    p = keep + send(give, CORE)
    keep = jnp.where(y == 0, p[:, 0], p[:, 1])
    give = jnp.where(y == 0, p[:, 1], p[:, 0])
    p = keep + send(give, YSWAP)
    planes = slots // 4
    total = lax.dynamic_index_in_dim(p, jnp.minimum(z, planes - 1), 0, keepdims=False)
    for d in (1, 2, 3):
        target = lax.rem(z + d, 4)
        block = lax.dynamic_index_in_dim(p, jnp.minimum(target, planes - 1), 0, keepdims=False)
        total = total + send_z(block, {s: (s + d) % 4 for s in range(4) if (s + d) % 4 < planes})

    rows = index * mine + lax.iota(jnp.int32, mine)
    cot_rows = lax.dynamic_slice_in_dim(
        jnp.pad(a_cot.T, ((mine, 0), (0, 0))), jnp.maximum(index * mine - 2 * RANK + mine, 0), mine, 0
    )
    summed = rows < 2 * RANK
    out_rows = jnp.where(summed[:, None], total, cot_rows)
    scale = 1.0 / math.sqrt(LEN)
    live = (lax.iota(jnp.int32, LEN)[None, :] < lengths[:, None]).astype(F32) * scale
    owner = jnp.eye(SEQS, dtype=F32)
    weights = (owner[:, :, None] * live[None]).reshape(SEQS, SEQS * LEN)
    left = (weights[:, None, :] * out_rows[None]).reshape(SEQS * mine, -1)
    sketch = jnp.dot(left, jnp.concatenate([a_in, a_hid], axis=1), precision=HIGHEST)
    sketch = sketch.reshape(SEQS, mine, 2 * RANK)
    sketch = jnp.where(summed[None, :, None], sketch[:, :, :RANK], sketch[:, :, RANK:])
    logged = sketch.reshape(SEQS, mine * RANK)
    stats = jnp.dot(jnp.concatenate([logged, queries], axis=0), logged.T, precision=HIGHEST)
    stats = sum_all(stats)
    scores = pl.pallas_call(
        solve_kernel, out_shape=jax.ShapeDtypeStruct((queries.shape[0], SEQS), F32)
    )(stats)
    return (logged, scores)


def solution(mesh):
    placed = (
        P(("group", "dp"), None),
        P(("group", "dp"), None),
        P("group"),
        P(None, "dp"),
        P(None, "dp"),
        P("dp", None),
        P(),
        P(),
        P("dp", None),
        P("dp", None),
        P("dp", None),
        P("group", "dp"),
    )
    return jax.shard_map(
        on_device_424 if mesh.shape["dp"] == 16 else on_device,
        mesh=mesh,
        in_specs=placed,
        out_specs=(P("group", "dp"), P("group", None)),
        check_vma=False,
    )
```

```python
import math

import jax
import jax.numpy as jnp
from jax import lax
from jax.experimental import pallas as pl
from jax.experimental.pallas import tpu as pltpu
from jax.sharding import PartitionSpec as P

RANK = 64
LEN = 64
SEQS = 8
HIGHEST = lax.Precision.HIGHEST
F32 = jnp.float32
BF16 = jnp.bfloat16


def silu_parts(gate):
    sigma = jax.nn.sigmoid(gate)
    return (gate * sigma, sigma * (1.0 + gate * (1.0 - sigma)))


def block_sketch(weight_rows, out_proj, in_proj):
    out_blocks = out_proj.reshape(SEQS, LEN, RANK)
    in_blocks = in_proj.reshape(SEQS, LEN, RANK)
    sketch = jnp.einsum(
        "sl,slo,sli->soi", weight_rows, out_blocks, in_blocks, precision=HIGHEST
    )
    return sketch.reshape(SEQS, RANK * RANK)


def on_device(
    tokens,
    cotangent,
    lengths,
    gate_weight,
    up_weight,
    down_weight,
    proj_input,
    proj_cotangent,
    proj_hidden,
    proj_up,
    proj_gate,
    queries,
):
    scale = 1.0 / math.sqrt(LEN)
    piece = lax.all_gather(tokens, "dp", axis=0, tiled=True)
    gate = jnp.dot(piece, gate_weight, preferred_element_type=F32)
    up = jnp.dot(piece, up_weight, preferred_element_type=F32)
    input_all = jnp.dot(piece, proj_input, preferred_element_type=F32)
    silu_val, silu_grad = silu_parts(gate)
    hidden = (silu_val * up).astype(BF16)
    piece = lax.all_gather(cotangent, "dp", axis=0, tiled=True)
    dhidden = lax.dot_general(
        piece, down_weight, (((1,), (1,)), ((), ())), preferred_element_type=F32
    )
    cot_all = jnp.dot(piece, proj_cotangent, preferred_element_type=F32)
    d_up = (dhidden * silu_val).astype(BF16)
    d_gate = (dhidden * up * silu_grad).astype(BF16)
    p_hid = jnp.dot(hidden, proj_hidden, preferred_element_type=F32)
    p_up = jnp.dot(d_up, proj_up, preferred_element_type=F32)
    p_gate = jnp.dot(d_gate, proj_gate, preferred_element_type=F32)
    a_hid, a_up, a_gate = lax.psum((p_hid, p_up, p_gate), "dp")
    live = (lax.iota(jnp.int32, LEN)[None, :] < lengths[:, None]).astype(F32) * scale
    logged = jnp.concatenate(
        [
            block_sketch(live, a_gate, input_all),
            block_sketch(live, a_up, input_all),
            block_sketch(live, cot_all, a_hid),
        ],
        axis=1,
    )
    width = queries.shape[1]
    logged_part = lax.dynamic_slice_in_dim(logged, lax.axis_index("dp") * width, width, 1)
    full_queries = lax.all_gather(queries, "dp", axis=1, tiled=True)
    gram = jnp.dot(logged, logged.T, precision=HIGHEST)
    cross = jnp.dot(full_queries, logged.T, precision=HIGHEST)
    damping = jnp.trace(gram) / SEQS
    system = gram + damping * jnp.eye(SEQS, dtype=F32)
    factor = jnp.linalg.cholesky(system)
    solved = jax.scipy.linalg.cho_solve((factor, True), cross.T)
    scores = damping * solved.T
    return (logged_part, scores)


PLACES = [(z, y, c) for z in range(4) for y in range(2) for c in range(2)]


def spot(z, y, c):
    return 4 * z + 2 * y + c


CORE = [(spot(z, y, c), spot(z, y, 1 - c)) for z, y, c in PLACES]
YSWAP = [(spot(z, y, c), spot(z, 1 - y, c)) for z, y, c in PLACES]
ZPAIR = [(spot(z, y, c), spot(z ^ 1, y, c)) for z, y, c in PLACES]
ZMID = [(spot(z, y, c), spot(3 - z, y, c)) for z, y, c in PLACES if z in (1, 2)]
ZOUT = [(spot(z, y, c), spot(z ^ 1, y, c)) for z, y, c in PLACES if z in (1, 2)]


def send(x, pairs):
    return lax.ppermute(x, "dp", pairs)


def send_z(x, targets):
    return send(x, [(spot(z, y, c), spot(targets[z], y, c)) for z, y, c in PLACES if z in targets])


def sum_all(x):
    x = x + send(x, CORE)
    x = x + send(x, YSWAP)
    parts = [send_z(x, {z: (z + d) % 4 for z in range(4)}) for d in (1, 2, 3)]
    return (x + parts[1]) + (parts[0] + parts[2])


def solve_kernel(stats_ref, out_ref):
    stats = stats_ref[...]
    gram = stats[:SEQS]
    row = lax.broadcasted_iota(jnp.int32, (SEQS, SEQS), 0)
    col = lax.broadcasted_iota(jnp.int32, (SEQS, SEQS), 1)
    eye = (row == col).astype(F32)
    damping = jnp.sum(gram * eye) / SEQS
    left = gram + damping * eye
    right = eye
    for k in range(SEQS):
        pivot = left[k : k + 1, k : k + 1]
        left_row = left[k : k + 1, :] / pivot
        right_row = right[k : k + 1, :] / pivot
        factor = jnp.where(row[:, :1] == k, 0.0, left[:, k : k + 1])
        left = jnp.where(row == k, left_row, left - factor * left_row)
        right = jnp.where(row == k, right_row, right - factor * right_row)
    cross = stats[SEQS:]
    out_ref[...] = damping * jnp.dot(cross, right, precision=HIGHEST, preferred_element_type=F32)


def tie(*arrays):
    return lax.optimization_barrier(arrays)


def dot(a, b):
    return jnp.dot(a, b, preferred_element_type=F32)


def dot_nt(a, b):
    return lax.dot_general(a, b, (((1,), (1,)), ((), ())), preferred_element_type=F32)


TILE = 256
DEPTH = 512
SPACE = 60 * 2**20


def pack_kernel(first_ref, last_ref, other_first_ref, other_last_ref, pick_ref, out_ref):
    rows = jnp.concatenate(
        [first_ref[...], last_ref[...], other_first_ref[...], other_last_ref[...]], axis=0
    )
    out_ref[...] = dot(pick_ref[...], rows).astype(BF16)


def pack(blocks, pick):
    live, width = pick.shape[0], blocks[0].shape[1]
    columns = 1024
    specs = [pl.BlockSpec((b.shape[0], columns), lambda i: (0, i)) for b in blocks]
    return pl.pallas_call(
        pack_kernel,
        grid=(width // columns,),
        in_specs=specs + [pl.BlockSpec(pick.shape, lambda i: (0, 0))],
        out_specs=pl.BlockSpec((live, columns), lambda i: (0, i)),
        out_shape=jax.ShapeDtypeStruct((live, width), BF16),
        cost_estimate=pl.CostEstimate(
            flops=2 * live * pick.shape[1] * width,
            bytes_accessed=2 * width * (live + pick.shape[1]),
            transcendentals=0,
        ),
    )(*blocks, pick)


def load_rows(x_ref, near_ref, far_refs, steps):
    slot = pl.program_id(0) // steps
    half = near_ref.shape[0]
    x_ref[:half] = near_ref[...]
    for s, far_ref in enumerate(far_refs):

        @pl.when(slot == s)
        def _():
            x_ref[half:] = far_ref[...]


def tiles(ref):
    return [slice(n, n + TILE) for n in range(0, ref.shape[1], TILE)]


def forward_kernel(steps, first, base_ref, near_ref, f0, f1, f2, f3, gate_w, up_w, proj_in, *refs):
    if first:
        gate_ref, up_ref, in_ref, x_ref = refs
    else:
        (gate_hbm, up_hbm, in_prev, proj_hid, gate_ref, up_ref, in_ref, hid_ref,
         x_ref, gate_prev, up_prev, sems) = refs
    step = pl.program_id(0)
    load_rows(x_ref, near_ref, (f0, f1, f2, f3), steps)
    if not first:
        copies = [
            pltpu.make_async_copy(gate_hbm, gate_prev, sems.at[0]),
            pltpu.make_async_copy(up_hbm, up_prev, sems.at[1]),
        ]

    @pl.when(step == 0)
    def _():
        gate_ref[...] = jnp.zeros_like(gate_ref)
        up_ref[...] = jnp.zeros_like(up_ref)
        in_ref[...] = jnp.zeros_like(in_ref) if first else in_prev[...]
        if not first:
            for copy in copies:
                copy.start()

    for cols in tiles(gate_ref):
        gate_ref[:, cols] += dot(x_ref[...], gate_w[:, cols])
        up_ref[:, cols] += dot(x_ref[...], up_w[:, cols])
    in_ref[...] += dot(x_ref[...], proj_in[...])

    if not first:

        @pl.when(step == pl.num_programs(0) - 1)
        def _():
            for copy in copies:
                copy.wait()
            total = jnp.zeros_like(hid_ref)
            for cols in tiles(gate_ref):
                silu_val, silu_grad = silu_parts(gate_ref[:, cols] + gate_prev[:, cols])
                up = up_ref[:, cols] + up_prev[:, cols]
                total += dot((silu_val * up).astype(BF16), proj_hid[cols, :])
                gate_ref[:, cols] = silu_val
                up_ref[:, cols] = up * silu_grad
            hid_ref[...] = total


def backward_kernel(steps, first, base_ref, near_ref, f0, f1, f2, f3, down_w, proj_cot, *refs):
    if first:
        dh_ref, cot_ref, x_ref = refs
    else:
        (dh_hbm, silu_hbm, grad_hbm, cot_prev, proj_gate, proj_up, gate_ref, up_ref, cot_ref,
         x_ref, dh_ref, dh_prev, silu_ref, grad_ref, sems) = refs
    step = pl.program_id(0)
    load_rows(x_ref, near_ref, (f0, f1, f2, f3), steps)
    if not first:
        copies = [
            pltpu.make_async_copy(dh_hbm, dh_prev, sems.at[0]),
            pltpu.make_async_copy(silu_hbm, silu_ref, sems.at[1]),
            pltpu.make_async_copy(grad_hbm, grad_ref, sems.at[2]),
        ]

    @pl.when(step == 0)
    def _():
        dh_ref[...] = jnp.zeros_like(dh_ref)
        cot_ref[...] = jnp.zeros_like(cot_ref) if first else cot_prev[...]
        if not first:
            for copy in copies:
                copy.start()

    for cols in tiles(dh_ref):
        dh_ref[:, cols] += dot_nt(x_ref[...], down_w[cols, :])
    cot_ref[...] += dot(x_ref[...], proj_cot[...])

    if not first:

        @pl.when(step == pl.num_programs(0) - 1)
        def _():
            for copy in copies:
                copy.wait()
            gate = jnp.zeros_like(gate_ref)
            up = jnp.zeros_like(up_ref)
            for cols in tiles(dh_ref):
                dhidden = dh_ref[:, cols] + dh_prev[:, cols]
                up += dot((dhidden * silu_ref[:, cols]).astype(BF16), proj_up[cols, :])
                gate += dot((dhidden * grad_ref[:, cols]).astype(BF16), proj_gate[cols, :])
            gate_ref[...] = gate
            up_ref[...] = up


def chunk_call(kernel, first, base, part, near, far, weights, proj, extra, extra_specs, outs, scratch, flops):
    live = near.shape[0]
    width = far[0].shape[1]
    depth = min(DEPTH, width)
    steps = width // depth
    share = near.shape[1] // 4 // depth
    every = lambda i, base: (0, 0)

    def place(i, base):
        return base[i // steps] * share + part * steps + i % steps

    def far_spec(s):
        return pl.BlockSpec(
            (live, depth), lambda i, base: (0, jnp.clip(i - s * steps, 0, steps - 1))
        )

    in_specs = [pl.BlockSpec((live, depth), lambda i, base: (0, place(i, base)))]
    in_specs += [far_spec(s) for s in range(4)]
    for w in weights:
        if w.shape[0] == near.shape[1]:
            in_specs.append(pl.BlockSpec((depth, w.shape[1]), lambda i, base: (place(i, base), 0)))
        else:
            in_specs.append(pl.BlockSpec((w.shape[0], depth), lambda i, base: (0, place(i, base))))
    in_specs.append(pl.BlockSpec((depth, proj.shape[1]), lambda i, base: (place(i, base), 0)))
    for kind, x in zip(extra_specs, extra):
        if kind == "any":
            in_specs.append(pl.BlockSpec(memory_space=pl.ANY))
        else:
            in_specs.append(pl.BlockSpec(x.shape, every, pipeline_mode=pl.Buffered(1)))
    size = 4 * steps * depth * sum(w.size // near.shape[1] for w in weights) * 2
    return pl.pallas_call(
        lambda *refs: kernel(steps, first, *refs),
        grid_spec=pltpu.PrefetchScalarGridSpec(
            num_scalar_prefetch=1,
            grid=(4 * steps,),
            in_specs=in_specs,
            out_specs=[pl.BlockSpec(o, every) for o in outs],
            scratch_shapes=[pltpu.VMEM((2 * live, depth), BF16)] + scratch,
        ),
        out_shape=[jax.ShapeDtypeStruct(o, F32) for o in outs],
        compiler_params=pltpu.CompilerParams(vmem_limit_bytes=SPACE),
        cost_estimate=pl.CostEstimate(flops=flops, bytes_accessed=size, transcendentals=0),
    )(base, near, *far, *weights, proj, *extra)


def forward_chunk(part, base, near, far, gate_weight, up_weight, proj_input, prev, proj_hidden):
    rows, cols = 2 * near.shape[0], gate_weight.shape[1]
    wide, thin = (rows, cols), (rows, RANK)
    flops = 2 * rows * cols * far[0].shape[1] * 4 * 2
    weights = (gate_weight, up_weight)
    if prev is None:
        return chunk_call(forward_kernel, True, base, part, near, far, weights, proj_input,
                          (), (), [wide, wide, thin], [], flops)
    extra = (*prev, proj_hidden)
    scratch = [pltpu.VMEM(wide, F32), pltpu.VMEM(wide, F32), pltpu.SemaphoreType.DMA((2,))]
    return chunk_call(forward_kernel, False, base, part, near, far, weights, proj_input,
                      extra, ("any", "any", "all", "all"), [wide, wide, thin, thin], scratch, flops)


def backward_chunk(part, base, near, far, down_weight, proj_cotangent, prev, silu, proj_gate, proj_up):
    rows, cols = 2 * near.shape[0], down_weight.shape[0]
    wide, thin = (rows, cols), (rows, RANK)
    flops = 2 * rows * cols * far[0].shape[1] * 4
    weights = (down_weight,)
    if prev is None:
        return chunk_call(backward_kernel, True, base, part, near, far, weights, proj_cotangent,
                          (), (), [wide, thin], [], flops)
    extra = (prev[0], *silu, prev[1], proj_gate, proj_up)
    scratch = [pltpu.VMEM(wide, F32)] * 4 + [pltpu.SemaphoreType.DMA((3,))]
    return chunk_call(backward_kernel, False, base, part, near, far, weights, proj_cotangent,
                      extra, ("any", "any", "any", "all", "all", "all"), [thin, thin, thin],
                      scratch, flops)


def sketch_kernel(far_first_ref, gate_ref, up_ref, cot_ref, in_ref, hid_ref, weight_ref, out_ref):
    live = gate_ref.shape[0] // 2
    far_first = far_first_ref[0]
    for half in range(2):
        rows = pl.ds(pl.multiple_of((far_first ^ half) * live, 16), live)
        outs = jnp.concatenate([gate_ref[rows], up_ref[rows], cot_ref[rows]], axis=1)
        ins = jnp.concatenate([in_ref[rows], hid_ref[rows]], axis=1)
        weight = weight_ref[rows]
        for k in range(SEQS // 2):
            s = half * (SEQS // 2) + k
            got = lax.dot_general(
                outs * weight[:, k : k + 1], ins, (((0,), (0,)), ((), ())),
                precision=HIGHEST, preferred_element_type=F32,
            )
            cols = slice(s * RANK, (s + 1) * RANK)
            out_ref[: 2 * RANK, cols] = got[: 2 * RANK, :RANK]
            out_ref[2 * RANK :, cols] = got[2 * RANK :, RANK:]


def half_layout(lengths, half):
    own = jnp.where(half == 0, lengths[: SEQS // 2], lengths[SEQS // 2 :])
    return own, jnp.cumsum(own) - own


def pick_rows(lengths, live, z, y, c):
    own, start = half_layout(lengths, z // 2)
    row = lax.iota(jnp.int32, 256)
    seq = ((row // 32) % 2 ^ (z % 2)) * 2 + ((row // 64) % 2 ^ y)
    token = (row // 128 ^ c) * 32 + row % 32
    place = jnp.full((256,), -1, jnp.int32)
    for s in range(SEQS // 2):
        place = jnp.where((seq == s) & (token < own[s]), start[s] + token, place)
    return (lax.iota(jnp.int32, live)[:, None] == place[None, :]).astype(BF16)


def row_weights(lengths, live, z):
    scale = 1.0 / math.sqrt(LEN)
    parts = []
    for block in range(2):
        own, start = half_layout(lengths, (z // 2) ^ block)
        at = lax.iota(jnp.int32, live)[:, None]
        inside = (at >= start[None]) & (at < (start + own)[None])
        parts.append(inside.astype(F32) * scale)
    return jnp.concatenate(parts, axis=0)


def share_of(packed, y, c):
    quarter = packed.shape[1] // 4
    return lax.dynamic_slice_in_dim(packed, (2 * y + c) * quarter, quarter, 1)


def packed_branch(live, index, lengths, tokens, tok_z, tok_y, cotangent, gate_weight, up_weight,
                  down_weight, proj_input, proj_cotangent, proj_hidden, proj_up, proj_gate, queries):
    z, y, c = index // 4, (index // 2) % 2, index % 2
    width = tokens.shape[1]
    half, piece = width // 2, width // 8
    is_mid = (z == 1) | (z == 2)
    pick = pick_rows(lengths, live, z, y, c)
    base = jnp.stack([2 * y + c, 2 * (1 - y) + c, 2 * y + 1 - c, 2 * (1 - y) + 1 - c]).astype(jnp.int32)

    def near_of(x, from_z, from_y, diag_z, diag_y):
        first = jnp.concatenate([x, from_z, from_y], axis=0)
        last = jnp.concatenate([diag_z, diag_y], axis=1)
        return pack((first, last, send(first, CORE), send(last, CORE)), pick)

    tok_dz, tok_dy = send(tok_y[:, :half], ZPAIR), send(tok_z[:, half:], YSWAP)
    cot_z, cot_y = send(cotangent, ZPAIR), send(cotangent, YSWAP)
    tok_near = near_of(tokens, tok_z, tok_y, tok_dz, tok_dy)
    tok_mid = send(share_of(tok_near, y, c), ZMID)
    cot_dz, cot_dy = send(cot_y[:, :half], ZPAIR), send(cot_z[:, half:], YSWAP)
    cot_near = near_of(cotangent, cot_z, cot_y, cot_dz, cot_dy)
    cot_mid = send(share_of(cot_near, y, c), ZMID)

    def cross(got, from_y):
        return (got, from_y, send(got, CORE), send(from_y, CORE))

    mids = [tok_mid[:, :piece], tok_mid[:, piece:], cot_mid[:, :piece], cot_mid[:, piece:]]
    far = []
    gots = []
    for k, mid in enumerate(mids):
        if k >= 1:
            mid, gots[-1] = tie(mid, gots[-1])
        outer = send(mid, ZOUT)
        gots.append(jnp.where(is_mid, mid, outer))
        if k >= 1:
            got = gots[k - 1]
            if far:
                got, far[-1] = tie(got, far[-1])
            far.append(send(got, YSWAP))
    got, far[-1] = tie(gots[-1], far[-1])
    far.append(send(got, YSWAP))
    sets = [cross(g, f) for g, f in zip(gots, far)]

    gate, up, a_in = forward_chunk(
        0, base, tok_near, sets[0], gate_weight, up_weight, proj_input, None, None)
    silu, grad, a_in, p_hid = forward_chunk(
        1, base, tok_near, sets[1], gate_weight, up_weight, proj_input, (gate, up, a_in), proj_hidden)
    dh, a_cot = backward_chunk(
        0, base, cot_near, sets[2], down_weight, proj_cotangent, None, None, None, None)
    p_gate, p_up, a_cot = backward_chunk(
        1, base, cot_near, sets[3], down_weight, proj_cotangent, (dh, a_cot), (silu, grad),
        proj_gate, proj_up)

    vmem = pl.BlockSpec(memory_space=pltpu.VMEM)
    partial = pl.pallas_call(
        sketch_kernel,
        in_specs=[pl.BlockSpec(memory_space=pltpu.SMEM)] + [vmem] * 6,
        out_specs=vmem,
        out_shape=jax.ShapeDtypeStruct((3 * RANK, SEQS * RANK), F32),
        compiler_params=pltpu.CompilerParams(vmem_limit_bytes=SPACE),
    )((z // 2).reshape(1), p_gate, p_up, a_cot, a_in, p_hid, row_weights(lengths, live, z))

    mine = 3 * RANK // 16
    p = partial.reshape(4, 2, 2, mine, SEQS * RANK)
    keep = jnp.where(c == 0, p[:, :, 0], p[:, :, 1])
    give = jnp.where(c == 0, p[:, :, 1], p[:, :, 0])
    p = keep + send(give, CORE)
    keep = jnp.where(y == 0, p[:, 0], p[:, 1])
    give = jnp.where(y == 0, p[:, 1], p[:, 0])
    p = keep + send(give, YSWAP)
    total = lax.dynamic_index_in_dim(p, z, 0, keepdims=False)
    for d in (1, 2, 3):
        block = lax.dynamic_index_in_dim(p, lax.rem(z + d, 4), 0, keepdims=False)
        total = total + send_z(block, {s: (s + d) % 4 for s in range(4)})
    logged = total.reshape(mine, SEQS, RANK).transpose(1, 0, 2).reshape(SEQS, mine * RANK)
    stats = jnp.dot(jnp.concatenate([logged, queries], axis=0), logged.T, precision=HIGHEST)
    stats = sum_all(stats)
    scores = pl.pallas_call(
        solve_kernel, out_shape=jax.ShapeDtypeStruct((queries.shape[0], SEQS), F32)
    )(stats)
    return (logged, scores)


SIZES = (128, 160, 192, 224, 256)


def on_device_424(
    tokens,
    cotangent,
    lengths,
    gate_weight,
    up_weight,
    down_weight,
    proj_input,
    proj_cotangent,
    proj_hidden,
    proj_up,
    proj_gate,
    queries,
):
    index = lax.axis_index("dp")
    halves = lengths.reshape(2, SEQS // 2).sum(axis=1)
    most = jnp.maximum(halves[0], halves[1])
    groups = lax.axis_size("group")
    for step in range(1, groups):
        turn = [(g, (g + step) % groups) for g in range(groups)]
        most = jnp.maximum(most, lax.ppermute(most, "group", turn))
    which = sum((most > size).astype(jnp.int32) for size in SIZES[:-1])
    tok_z, tok_y = send(tokens, ZPAIR), send(tokens, YSWAP)
    which, tok_z, tok_y = tie(which, tok_z, tok_y)
    branches = [lambda *args, live=live: packed_branch(live, *args) for live in SIZES]
    return lax.switch(
        which, branches, index, lengths, tokens, tok_z, tok_y, cotangent, gate_weight, up_weight,
        down_weight, proj_input, proj_cotangent, proj_hidden, proj_up, proj_gate, queries
    )


def solution(mesh):
    placed = (
        P(("group", "dp"), None),
        P(("group", "dp"), None),
        P("group"),
        P(None, "dp"),
        P(None, "dp"),
        P("dp", None),
        P(),
        P(),
        P("dp", None),
        P("dp", None),
        P("dp", None),
        P("group", "dp"),
    )
    return jax.shard_map(
        on_device_424 if mesh.shape["dp"] == 16 else on_device,
        mesh=mesh,
        in_specs=placed,
        out_specs=(P("group", "dp"), P("group", None)),
        check_vma=False,
    )
```

```python
import math

import jax
import jax.numpy as jnp
from jax import lax
from jax.experimental import pallas as pl
from jax.experimental.pallas import tpu as pltpu
from jax.sharding import PartitionSpec as P

RANK = 64
LEN = 64
SEQS = 8
HIGHEST = lax.Precision.HIGHEST
F32 = jnp.float32
BF16 = jnp.bfloat16


def silu_parts(gate):
    sigma = jax.nn.sigmoid(gate)
    return (gate * sigma, sigma * (1.0 + gate * (1.0 - sigma)))


def block_sketch(weight_rows, out_proj, in_proj):
    out_blocks = out_proj.reshape(SEQS, LEN, RANK)
    in_blocks = in_proj.reshape(SEQS, LEN, RANK)
    sketch = jnp.einsum(
        "sl,slo,sli->soi", weight_rows, out_blocks, in_blocks, precision=HIGHEST
    )
    return sketch.reshape(SEQS, RANK * RANK)


def on_device(
    tokens,
    cotangent,
    lengths,
    gate_weight,
    up_weight,
    down_weight,
    proj_input,
    proj_cotangent,
    proj_hidden,
    proj_up,
    proj_gate,
    queries,
):
    scale = 1.0 / math.sqrt(LEN)
    piece = lax.all_gather(tokens, "dp", axis=0, tiled=True)
    gate = jnp.dot(piece, gate_weight, preferred_element_type=F32)
    up = jnp.dot(piece, up_weight, preferred_element_type=F32)
    input_all = jnp.dot(piece, proj_input, preferred_element_type=F32)
    silu_val, silu_grad = silu_parts(gate)
    hidden = (silu_val * up).astype(BF16)
    piece = lax.all_gather(cotangent, "dp", axis=0, tiled=True)
    dhidden = lax.dot_general(
        piece, down_weight, (((1,), (1,)), ((), ())), preferred_element_type=F32
    )
    cot_all = jnp.dot(piece, proj_cotangent, preferred_element_type=F32)
    d_up = (dhidden * silu_val).astype(BF16)
    d_gate = (dhidden * up * silu_grad).astype(BF16)
    p_hid = jnp.dot(hidden, proj_hidden, preferred_element_type=F32)
    p_up = jnp.dot(d_up, proj_up, preferred_element_type=F32)
    p_gate = jnp.dot(d_gate, proj_gate, preferred_element_type=F32)
    a_hid, a_up, a_gate = lax.psum((p_hid, p_up, p_gate), "dp")
    live = (lax.iota(jnp.int32, LEN)[None, :] < lengths[:, None]).astype(F32) * scale
    logged = jnp.concatenate(
        [
            block_sketch(live, a_gate, input_all),
            block_sketch(live, a_up, input_all),
            block_sketch(live, cot_all, a_hid),
        ],
        axis=1,
    )
    width = queries.shape[1]
    logged_part = lax.dynamic_slice_in_dim(logged, lax.axis_index("dp") * width, width, 1)
    full_queries = lax.all_gather(queries, "dp", axis=1, tiled=True)
    gram = jnp.dot(logged, logged.T, precision=HIGHEST)
    cross = jnp.dot(full_queries, logged.T, precision=HIGHEST)
    damping = jnp.trace(gram) / SEQS
    system = gram + damping * jnp.eye(SEQS, dtype=F32)
    factor = jnp.linalg.cholesky(system)
    solved = jax.scipy.linalg.cho_solve((factor, True), cross.T)
    scores = damping * solved.T
    return (logged_part, scores)


PLACES = [(z, y, c) for z in range(4) for y in range(2) for c in range(2)]


def spot(z, y, c):
    return 4 * z + 2 * y + c


CORE = [(spot(z, y, c), spot(z, y, 1 - c)) for z, y, c in PLACES]
YSWAP = [(spot(z, y, c), spot(z, 1 - y, c)) for z, y, c in PLACES]
ZPAIR = [(spot(z, y, c), spot(z ^ 1, y, c)) for z, y, c in PLACES]
ZFAR = [(spot(z, y, c), spot(z ^ 2, y, c)) for z, y, c in PLACES]


def send(x, pairs):
    return lax.ppermute(x, "dp", pairs)


def solve_kernel(stats_ref, out_ref):
    stats = stats_ref[...]
    gram = stats[:SEQS]
    row = lax.broadcasted_iota(jnp.int32, (SEQS, SEQS), 0)
    col = lax.broadcasted_iota(jnp.int32, (SEQS, SEQS), 1)
    eye = (row == col).astype(F32)
    damping = jnp.sum(gram * eye) / SEQS
    left = gram + damping * eye
    right = eye
    for k in range(SEQS):
        pivot = left[k : k + 1, k : k + 1]
        left_row = left[k : k + 1, :] / pivot
        right_row = right[k : k + 1, :] / pivot
        factor = jnp.where(row[:, :1] == k, 0.0, left[:, k : k + 1])
        left = jnp.where(row == k, left_row, left - factor * left_row)
        right = jnp.where(row == k, right_row, right - factor * right_row)
    cross = stats[SEQS:]
    out_ref[...] = damping * jnp.dot(cross, right, precision=HIGHEST, preferred_element_type=F32)


def tie(*arrays):
    return lax.optimization_barrier(arrays)


def dot(a, b):
    return jnp.dot(a, b, preferred_element_type=F32)


def dot_nt(a, b):
    return lax.dot_general(a, b, (((1,), (1,)), ((), ())), preferred_element_type=F32)


TILE = 256
SPACE = 32 * 2**20


def group_lengths(lengths_ref, half):
    own = [lengths_ref[half * (SEQS // 2) + s] for s in range(SEQS // 2)]
    start = [0]
    for length in own[:-1]:
        start.append(start[-1] + length)
    return own, start


def packed_places(index, lengths_ref):
    z, y, c = index // 4, (index // 2) % 2, index % 2
    own, start = group_lengths(lengths_ref, z // 2)
    row = lax.broadcasted_iota(jnp.int32, (1, 256), 1)
    seq = ((row // 32) % 2 ^ (z % 2)) * 2 + ((row // 64) % 2 ^ y)
    token = (row // 128 ^ c) * 32 + row % 32
    place = jnp.full((1, 256), -1, jnp.int32)
    for s in range(SEQS // 2):
        place = jnp.where((seq == s) & (token < own[s]), start[s] + token, place)
    return place


def pack(index, lengths, pieces, live, quarter_only, after=None):
    width = pieces[0].shape[1]
    columns = width // 8 if quarter_only else width // 4
    steps = 2 if quarter_only else 4
    middle = width // columns // 2
    outs = 2 if quarter_only else 1

    def at(i, index_ref):
        return (index_ref[0] % 4) * 2 + i if quarter_only else i

    def kernel(index_ref, lengths_ref, *refs):
        pick_ref, rows_ref = refs[-2:]
        out_refs = refs[-2 - outs : -2]

        @pl.when(pl.program_id(0) == 0)
        def _():
            row = lax.broadcasted_iota(jnp.int32, (live, 256), 0)
            place = packed_places(index_ref[0], lengths_ref)
            pick_ref[...] = (row == place).astype(F32).astype(BF16)

        low = at(pl.program_id(0), index_ref) < middle
        for k, x in enumerate(refs[:10]):
            rows = slice(128 * (k // 5) + 32 * min(k % 5, 3), 128 * (k // 5) + 32 * min(k % 5, 3) + 32)
            if k % 5 < 3:
                rows_ref[rows] = x[...]
            elif k % 5 == 3:
                rows_ref[rows] = jnp.where(low, x[...], refs[k + 1][...])
        got = dot(pick_ref[...], rows_ref[...]).astype(BF16)
        if not quarter_only:
            out_refs[0][...] = got
        for k in range(outs if quarter_only else 0):

            @pl.when(pl.program_id(0) == k)
            def _():
                out_refs[k][...] = got

    specs = []
    for k, x in enumerate(pieces):
        last = x.shape[1] // columns - 1
        if k % 5 == 3:
            place = lambda i, q, n, last=last: (0, jnp.minimum(at(i, q), last))
        elif k % 5 == 4:
            place = lambda i, q, n, last=last: (0, jnp.maximum(at(i, q) - last - 1, 0))
        else:
            place = lambda i, q, n: (0, at(i, q))
        specs.append(pl.BlockSpec((32, columns), place))
    extra = () if after is None else (after,)
    return pl.pallas_call(
        kernel,
        grid_spec=pltpu.PrefetchScalarGridSpec(
            num_scalar_prefetch=2,
            grid=(steps,),
            in_specs=specs + [pl.BlockSpec(memory_space=pl.ANY)] * len(extra),
            out_specs=[
                pl.BlockSpec((live, columns), lambda i, q, n: (0, 0 if quarter_only else i))
            ] * outs,
            scratch_shapes=[pltpu.VMEM((live, 256), BF16), pltpu.VMEM((256, columns), BF16)],
        ),
        out_shape=[jax.ShapeDtypeStruct((live, columns if quarter_only else width), BF16)] * outs,
        compiler_params=pltpu.CompilerParams(vmem_limit_bytes=SPACE),
        cost_estimate=pl.CostEstimate(
            flops=2 * live * 256 * steps * columns,
            bytes_accessed=2 * steps * columns * (live + 256),
            transcendentals=0,
        ),
    )(index, lengths, *pieces, *extra)


TURNS = (0, 2, 1, 3)


def load_rows(index_ref, near, far, x_ref, sems):
    live = x_ref.shape[0] // 2

    @pl.when(pl.program_id(0) == 0)
    def _():
        copies = [pltpu.make_async_copy(near, x_ref.at[:live], sems.at[0])]
        quarter = lax.rem(index_ref[0], 4)
        for k, block in enumerate(far):
            piece = block.shape[1]
            at = ((quarter ^ TURNS[k % 4]) * (len(far) // 4) + k // 4) * piece
            cols = pl.ds(pl.multiple_of(at, piece), piece)
            copies.append(pltpu.make_async_copy(block, x_ref.at[live:, cols], sems.at[1 + k]))
        for copy in copies:
            copy.start()
        for copy in copies:
            copy.wait()


def add_share(steps, out_ref, x_ref, proj_ref):
    step = pl.program_id(0)
    shares = 4 if steps >= 4 else 2 if steps >= 2 else 1
    depth = x_ref.shape[1] // shares
    at = pl.ds(pl.multiple_of(lax.rem(step, shares) * depth, depth), depth)

    @pl.when(step < shares)
    def _():
        part = dot_nt(x_ref[:, at], proj_ref[:, at])
        out_ref[...] = jnp.where(step == 0, part, out_ref[...] + part)


def forward_kernel(pieces, steps, first, index_ref, *refs):
    blocks, refs = refs[:pieces], refs[pieces:]
    gate_w, up_w, proj_hid, *refs = refs
    if first:
        proj_in, silu_ref, grad_ref, hid_ref, in_ref, x_ref, sems = refs
    else:
        _, _, hid_prev, silu_ref, grad_ref, hid_ref, x_ref, sems = refs
    load_rows(index_ref, blocks[0], blocks[1:], x_ref, sems)
    if first:
        add_share(steps, in_ref, x_ref, proj_in)
    silu_val, silu_grad = silu_parts(dot(x_ref[...], gate_w[...]))
    up = dot(x_ref[...], up_w[...])
    silu_ref[...] = silu_val
    grad_ref[...] = up * silu_grad
    part = dot_nt((silu_val * up).astype(BF16), proj_hid[...])
    before = jnp.zeros_like(part) if first else hid_prev[...]
    hid_ref[...] = jnp.where(pl.program_id(0) == 0, before, hid_ref[...]) + part


def backward_kernel(pieces, steps, index_ref, *refs):
    blocks, refs = refs[:pieces], refs[pieces:]
    down_w, proj_cot, silu_ref, grad_ref, proj_gate, proj_up, *refs = refs
    gate_ref, up_ref, cot_ref, x_ref, sems = refs
    load_rows(index_ref, blocks[0], blocks[1:], x_ref, sems)
    add_share(steps, cot_ref, x_ref, proj_cot)
    dhidden = dot_nt(x_ref[...], down_w[...])
    up = dot_nt((dhidden * silu_ref[...]).astype(BF16), proj_up[...])
    gate = dot_nt((dhidden * grad_ref[...]).astype(BF16), proj_gate[...])
    first = pl.program_id(0) == 0
    up_ref[...] = jnp.where(first, up, up_ref[...] + up)
    gate_ref[...] = jnp.where(first, gate, gate_ref[...] + gate)


def rows_call(kernel, tiles, index, rows, width, blocks, specs, operands, outs, work, aliases):
    start, stop = tiles
    anywhere = pl.BlockSpec(memory_space=pl.ANY)
    kinds = {
        "wide": lambda shape: pl.BlockSpec((shape[0], TILE), lambda n, i: (0, start + n)),
        "down": lambda shape: pl.BlockSpec((width, TILE), lambda n, i: (0, start + n)),
        "across": lambda shape: pl.BlockSpec((TILE, width), lambda n, i: (start + n, 0)),
        "side": lambda shape: pl.BlockSpec((RANK, TILE), lambda n, i: (0, start + n)),
        "whole": lambda shape: pl.BlockSpec(shape, lambda n, i: (0, 0)),
        "any": lambda shape: anywhere,
    }
    return pl.pallas_call(
        kernel,
        grid_spec=pltpu.PrefetchScalarGridSpec(
            num_scalar_prefetch=1,
            grid=(stop - start,),
            in_specs=[anywhere] * len(blocks) + [kinds[s](x.shape) for s, x in zip(specs, operands)],
            out_specs=[kinds[s](o) for s, o in outs],
            scratch_shapes=[pltpu.VMEM((rows, width), BF16), pltpu.SemaphoreType.DMA((1 + len(blocks),))],
        ),
        out_shape=[jax.ShapeDtypeStruct(o, F32) for _, o in outs],
        input_output_aliases=aliases,
        compiler_params=pltpu.CompilerParams(vmem_limit_bytes=SPACE),
        cost_estimate=pl.CostEstimate(
            flops=2 * rows * width * (stop - start) * TILE * work,
            bytes_accessed=2 * width * (stop - start) * TILE * work,
            transcendentals=0,
        ),
    )(index, *blocks, *operands)


def forward_part(tiles, index, blocks, gate_weight, up_weight, proj_hidden, proj_input, prev):
    width, cols = gate_weight.shape
    rows = 2 * blocks[0].shape[0]
    first = prev is None
    specs = ["down", "down", "side"] + (["whole"] if first else ["any", "any", "whole"])
    operands = [gate_weight, up_weight, proj_hidden] + ([proj_input] if first else list(prev))
    outs = [("wide", (rows, cols))] * 2 + [("whole", (rows, RANK))] * (2 if first else 1)
    before = 1 + len(blocks) + 3
    aliases = {} if first else {before: 0, before + 1: 1}
    kernel = lambda *refs: forward_kernel(len(blocks), tiles[1] - tiles[0], first, *refs)
    return rows_call(kernel, tiles, index, rows, width, blocks, specs, operands, outs, 2, aliases)


def backward_part(index, near, far, down_weight, proj_cotangent, silu, grad, proj_gate, proj_up):
    cols, width = down_weight.shape
    rows = 2 * near.shape[0]
    specs = ["across", "whole"] + ["wide"] * 2 + ["side", "side"]
    operands = [down_weight, proj_cotangent, silu, grad, proj_gate, proj_up]
    kernel = lambda *refs: backward_kernel(1 + len(far), cols // TILE, *refs)
    return rows_call(kernel, (0, cols // TILE), index, rows, width, (near, *far), specs, operands,
                     [("whole", (rows, RANK))] * 3, 1, {})


MINE = 3 * RANK // 16


def sketch_kernel(index_ref, lengths_ref, gate_ref, up_ref, cot_ref, in_ref, hid_ref, keep_ref, give_ref, even_ref, odd_ref):
    live = gate_ref.shape[0] // 2
    far_first = index_ref[0] // 8
    scale = 1.0 / math.sqrt(LEN)
    at = lax.broadcasted_iota(jnp.int32, (live, 1), 0)
    for half in range(2):
        own, start = group_lengths(lengths_ref, half)
        rows = pl.ds(pl.multiple_of((far_first ^ half) * live, 16), live)
        outs = jnp.concatenate([gate_ref[rows], up_ref[rows], cot_ref[rows]], axis=1)
        ins = jnp.concatenate([in_ref[rows], hid_ref[rows]], axis=1)
        for k in range(SEQS // 2):
            s = half * (SEQS // 2) + k
            weight = jnp.where((at >= start[k]) & (at < start[k] + own[k]), scale, 0.0)
            got = lax.dot_general(
                outs * weight, ins, (((0,), (0,)), ((), ())),
                precision=HIGHEST, preferred_element_type=F32,
            )
            cols = slice(s * RANK, (s + 1) * RANK)
            got = jnp.concatenate([got[: 2 * RANK, :RANK], got[2 * RANK :, RANK:]], axis=0)
            for place in range(16):
                z, y, c = place // 4, (place // 2) % 2, place % 2
                at_row = (4 * y + z) * MINE
                rows_of = got[place * MINE : (place + 1) * MINE]
                (odd_ref if c else even_ref)[at_row : at_row + MINE, cols] = rows_of
    odd = lax.rem(index_ref[0], 2) == 1
    keep_ref[...] = jnp.where(odd, odd_ref[...], even_ref[...])
    give_ref[...] = jnp.where(odd, even_ref[...], odd_ref[...])


def packed_branch(live, index, lengths, tokens, cotangent, gate_weight, up_weight, down_weight,
                  proj_input, proj_cotangent, proj_hidden, proj_up, proj_gate, queries):
    z, y, c = index // 4, (index // 2) % 2, index % 2
    width = tokens.shape[1]
    half, piece = width // 2, width // 8
    index_ref = index.reshape(1)

    tok_z, tok_y = send(tokens, ZPAIR), send(tokens, YSWAP)
    tok_core = send(tokens, CORE)
    tok_dz, tok_dy = send(tok_y[:, :half], ZPAIR), send(tok_z[:, half:], YSWAP)
    tok_pieces = (tokens, tok_z, tok_y, tok_dz, tok_dy, tok_core) + tuple(
        send(x, CORE) for x in (tok_z, tok_y, tok_dz, tok_dy))
    first_0, first_1 = pack(index_ref, lengths, tok_pieces, live, True)
    got_0, got_1 = send(first_0, ZFAR), send(first_1, ZFAR)
    cotangent, first_0 = tie(cotangent, first_0)
    cot_z, cot_y = send(cotangent, ZPAIR), send(cotangent, YSWAP)
    cot_dz, cot_dy = send(cot_y[:, :half], ZPAIR), send(cot_z[:, half:], YSWAP)
    cot_pieces = (cotangent, cot_z, cot_y, cot_dz, cot_dy)
    cot_pieces += tuple(send(x, CORE) for x in cot_pieces)
    first_2, first_3 = pack(index_ref, lengths, cot_pieces, live, True, after=first_0)
    got_2, got_3 = send(first_2, ZFAR), send(first_3, ZFAR)

    def cross(got, from_y):
        return (got, from_y, send(got, CORE), send(from_y, CORE))

    (tok_near,) = pack(index_ref, lengths, tok_pieces, live, False, after=first_0)
    got_0, tok_near = tie(got_0, tok_near)
    far_0 = send(got_0, YSWAP)
    far_1 = send(got_1, YSWAP)
    far_1, first_2 = tie(far_1, first_2)
    tok_far = cross(got_0, far_0) + cross(got_1, far_1)
    queries, got_1 = tie(queries, got_1)
    other = send(queries, ZPAIR)
    pair = jnp.where(z % 2 == 0, jnp.concatenate([queries, other], 1), jnp.concatenate([other, queries], 1))
    other = send(pair, ZFAR)
    all_queries = jnp.where(z // 2 == 0, jnp.concatenate([pair, other], 1), jnp.concatenate([other, pair], 1))

    turned = (proj_hidden.T, proj_input.T)
    tiles = gate_weight.shape[1] // TILE
    cut = -(-tiles // 2)
    forward = lambda part, prev: forward_part(
        part, index_ref, (tok_near, *tok_far), gate_weight, up_weight, *turned, prev)
    silu, grad, p_hid, a_in = forward((0, cut), None)
    (cot_near,) = pack(index_ref, lengths, cot_pieces, live, False, after=p_hid)
    got_2, got_3, p_hid, cot_near = tie(got_2, got_3, p_hid, cot_near)
    far_2, far_3 = send(got_2, YSWAP), send(got_3, YSWAP)
    silu, grad, p_hid = forward((cut, tiles), (silu, grad, p_hid))
    far_2, far_3, p_hid, all_queries = tie(far_2, far_3, p_hid, all_queries)
    cot_far = cross(got_2, far_2) + cross(got_3, far_3)
    p_gate, p_up, a_cot = backward_part(
        index_ref, cot_near, cot_far, down_weight, proj_cotangent.T, silu, grad, proj_gate.T, proj_up.T)

    vmem, smem = pl.BlockSpec(memory_space=pltpu.VMEM), pl.BlockSpec(memory_space=pltpu.SMEM)
    rows = 8 * MINE
    flat = jax.ShapeDtypeStruct((rows, SEQS * RANK), F32)
    keep, give = pl.pallas_call(
        sketch_kernel,
        in_specs=[smem] * 2 + [vmem] * 5,
        out_specs=[vmem] * 2,
        out_shape=[flat] * 2,
        scratch_shapes=[pltpu.VMEM(flat.shape, F32)] * 2,
        compiler_params=pltpu.CompilerParams(vmem_limit_bytes=SPACE),
    )(index_ref, lengths, p_gate, p_up, a_cot, a_in, p_hid)
    p = keep + send(give, CORE)
    low, high = p[: rows // 2], p[rows // 2 :]
    p = jnp.where(y == 0, low, high) + send(jnp.where(y == 0, high, low), YSWAP)
    p = p + send(p, ZPAIR)
    p = p + send(p, ZFAR)
    total = lax.dynamic_slice_in_dim(p, z * MINE, MINE, 0)
    logged = total.reshape(MINE, SEQS, RANK).transpose(1, 0, 2).reshape(SEQS, MINE * RANK)
    lines = p.reshape(4 * MINE, SEQS, RANK).transpose(1, 0, 2).reshape(SEQS, 4 * MINE * RANK)
    stats = jnp.dot(jnp.concatenate([lines, all_queries], axis=0), lines.T, precision=HIGHEST)
    stats = stats + send(stats, CORE)
    stats = stats + send(stats, YSWAP)
    scores = pl.pallas_call(
        solve_kernel, out_shape=jax.ShapeDtypeStruct((queries.shape[0], SEQS), F32)
    )(stats)
    return (logged, scores)


SIZES = (128, 160, 176, 192, 224, 256)


def on_device_424(
    tokens,
    cotangent,
    lengths,
    gate_weight,
    up_weight,
    down_weight,
    proj_input,
    proj_cotangent,
    proj_hidden,
    proj_up,
    proj_gate,
    queries,
):
    index = lax.axis_index("dp")
    halves = lengths.reshape(2, SEQS // 2).sum(axis=1)
    most = jnp.maximum(halves[0], halves[1])
    which = sum((most > size).astype(jnp.int32) for size in SIZES[:-1])
    branches = [lambda *args, live=live: packed_branch(live, *args) for live in SIZES]
    return lax.switch(
        which, branches, index, lengths, tokens, cotangent, gate_weight, up_weight, down_weight,
        proj_input, proj_cotangent, proj_hidden, proj_up, proj_gate, queries
    )


def solution(mesh):
    placed = (
        P(("group", "dp"), None),
        P(("group", "dp"), None),
        P("group"),
        P(None, "dp"),
        P(None, "dp"),
        P("dp", None),
        P(),
        P(),
        P("dp", None),
        P("dp", None),
        P("dp", None),
        P("group", "dp"),
    )
    return jax.shard_map(
        on_device_424 if mesh.shape["dp"] == 16 else on_device,
        mesh=mesh,
        in_specs=placed,
        out_specs=(P("group", "dp"), P("group", None)),
        check_vma=False,
    )
```

```python
import math

import jax
import jax.numpy as jnp
from jax import lax
from jax.experimental import pallas as pl
from jax.experimental.pallas import tpu as pltpu
from jax.sharding import PartitionSpec as P

RANK = 64
LEN = 64
SEQS = 8
HIGHEST = lax.Precision.HIGHEST
F32 = jnp.float32
BF16 = jnp.bfloat16


def silu_parts(gate):
    sigma = jax.nn.sigmoid(gate)
    return (gate * sigma, sigma * (1.0 + gate * (1.0 - sigma)))


def block_sketch(weight_rows, out_proj, in_proj):
    out_blocks = out_proj.reshape(SEQS, LEN, RANK)
    in_blocks = in_proj.reshape(SEQS, LEN, RANK)
    sketch = jnp.einsum(
        "sl,slo,sli->soi", weight_rows, out_blocks, in_blocks, precision=HIGHEST
    )
    return sketch.reshape(SEQS, RANK * RANK)


def on_device(
    tokens,
    cotangent,
    lengths,
    gate_weight,
    up_weight,
    down_weight,
    proj_input,
    proj_cotangent,
    proj_hidden,
    proj_up,
    proj_gate,
    queries,
):
    scale = 1.0 / math.sqrt(LEN)
    piece = lax.all_gather(tokens, "dp", axis=0, tiled=True)
    gate = jnp.dot(piece, gate_weight, preferred_element_type=F32)
    up = jnp.dot(piece, up_weight, preferred_element_type=F32)
    input_all = jnp.dot(piece, proj_input, preferred_element_type=F32)
    silu_val, silu_grad = silu_parts(gate)
    hidden = (silu_val * up).astype(BF16)
    piece = lax.all_gather(cotangent, "dp", axis=0, tiled=True)
    dhidden = lax.dot_general(
        piece, down_weight, (((1,), (1,)), ((), ())), preferred_element_type=F32
    )
    cot_all = jnp.dot(piece, proj_cotangent, preferred_element_type=F32)
    d_up = (dhidden * silu_val).astype(BF16)
    d_gate = (dhidden * up * silu_grad).astype(BF16)
    p_hid = jnp.dot(hidden, proj_hidden, preferred_element_type=F32)
    p_up = jnp.dot(d_up, proj_up, preferred_element_type=F32)
    p_gate = jnp.dot(d_gate, proj_gate, preferred_element_type=F32)
    a_hid, a_up, a_gate = lax.psum((p_hid, p_up, p_gate), "dp")
    live = (lax.iota(jnp.int32, LEN)[None, :] < lengths[:, None]).astype(F32) * scale
    logged = jnp.concatenate(
        [
            block_sketch(live, a_gate, input_all),
            block_sketch(live, a_up, input_all),
            block_sketch(live, cot_all, a_hid),
        ],
        axis=1,
    )
    width = queries.shape[1]
    logged_part = lax.dynamic_slice_in_dim(logged, lax.axis_index("dp") * width, width, 1)
    full_queries = lax.all_gather(queries, "dp", axis=1, tiled=True)
    gram = jnp.dot(logged, logged.T, precision=HIGHEST)
    cross = jnp.dot(full_queries, logged.T, precision=HIGHEST)
    damping = jnp.trace(gram) / SEQS
    system = gram + damping * jnp.eye(SEQS, dtype=F32)
    factor = jnp.linalg.cholesky(system)
    solved = jax.scipy.linalg.cho_solve((factor, True), cross.T)
    scores = damping * solved.T
    return (logged_part, scores)


PLACES = [(z, y, c) for z in range(4) for y in range(2) for c in range(2)]


def spot(z, y, c):
    return 4 * z + 2 * y + c


CORE = [(spot(z, y, c), spot(z, y, 1 - c)) for z, y, c in PLACES]
YSWAP = [(spot(z, y, c), spot(z, 1 - y, c)) for z, y, c in PLACES]
ZPAIR = [(spot(z, y, c), spot(z ^ 1, y, c)) for z, y, c in PLACES]
ZFAR = [(spot(z, y, c), spot(z ^ 2, y, c)) for z, y, c in PLACES]


def send(x, pairs):
    return lax.ppermute(x, "dp", pairs)


def solve_kernel(stats_ref, out_ref):
    stats = stats_ref[...]
    gram = stats[:SEQS]
    row = lax.broadcasted_iota(jnp.int32, (SEQS, SEQS), 0)
    col = lax.broadcasted_iota(jnp.int32, (SEQS, SEQS), 1)
    eye = (row == col).astype(F32)
    damping = jnp.sum(gram * eye) / SEQS
    left = gram + damping * eye
    right = eye
    for k in range(SEQS):
        pivot = left[k : k + 1, k : k + 1]
        left_row = left[k : k + 1, :] / pivot
        right_row = right[k : k + 1, :] / pivot
        factor = jnp.where(row[:, :1] == k, 0.0, left[:, k : k + 1])
        left = jnp.where(row == k, left_row, left - factor * left_row)
        right = jnp.where(row == k, right_row, right - factor * right_row)
    cross = stats[SEQS:]
    out_ref[...] = damping * jnp.dot(cross, right, precision=HIGHEST, preferred_element_type=F32)


def tie(*arrays):
    return lax.optimization_barrier(arrays)


def dot(a, b):
    return jnp.dot(a, b, preferred_element_type=F32)


def dot_nt(a, b):
    return lax.dot_general(a, b, (((1,), (1,)), ((), ())), preferred_element_type=F32)


TILE = 256
SPACE = 32 * 2**20


def group_lengths(lengths_ref, half):
    own = [lengths_ref[half * (SEQS // 2) + s] for s in range(SEQS // 2)]
    start = [0]
    for length in own[:-1]:
        start.append(start[-1] + length)
    return own, start


def packed_places(index, lengths_ref):
    z, y, c = index // 4, (index // 2) % 2, index % 2
    own, start = group_lengths(lengths_ref, z // 2)
    row = lax.broadcasted_iota(jnp.int32, (1, 256), 1)
    seq = ((row // 32) % 2 ^ (z % 2)) * 2 + ((row // 64) % 2 ^ y)
    token = (row // 128 ^ c) * 32 + row % 32
    place = jnp.full((1, 256), -1, jnp.int32)
    for s in range(SEQS // 2):
        place = jnp.where((seq == s) & (token < own[s]), start[s] + token, place)
    return place


def pack(index, lengths, pieces, live, quarter_only, after=None, outs=1):
    width = pieces[0].shape[1]
    columns = width // 4
    chunks = 1 if quarter_only else 4

    def kernel(index_ref, lengths_ref, *refs):
        blocks, refs = refs[:10], refs[10 + (after is not None) :]
        out_refs, (pick_ref, rows_ref, sems) = refs[:outs], refs[outs:]

        def copy(chunk, k, source):
            rows = pl.ds(128 * (k // 5) + 32 * min(k % 5, 3), 32)
            cols = pl.ds(chunk * columns, columns)
            return pltpu.make_async_copy(source, rows_ref.at[rows, cols], sems.at[chunk, k])

        def part(block, at):
            if not isinstance(at, int):
                at = pl.multiple_of(at, columns)
            return block.at[:, pl.ds(at, columns)]

        for chunk in range(chunks):
            quarter = lax.rem(index_ref[0], 4) if quarter_only else chunk
            for k in (0, 1, 2, 5, 6, 7):
                copy(chunk, k, part(blocks[k], quarter * columns)).start()
            for k in (3, 8):
                if not quarter_only:
                    block = blocks[k + quarter // 2]
                    copy(chunk, k, part(block, quarter % 2 * columns)).start()
                else:
                    for side in range(2):

                        @pl.when(quarter // 2 == side)
                        def _():
                            at = lax.rem(quarter, 2) * columns
                            copy(chunk, k, part(blocks[k + side], at)).start()

        row = lax.broadcasted_iota(jnp.int32, (live, 256), 0)
        place = packed_places(index_ref[0], lengths_ref)
        pick_ref[...] = (row == place).astype(F32).astype(BF16)
        for chunk in range(chunks):
            for k in (0, 1, 2, 3, 5, 6, 7, 8):
                copy(chunk, k, part(blocks[k], 0)).wait()
            cols = slice(chunk * columns, (chunk + 1) * columns)
            got = dot(pick_ref[...], rows_ref[:, cols]).astype(BF16)
            if outs == 1:
                out_refs[0][:, cols] = got
            else:
                for k in range(outs):
                    out_refs[k][...] = got[:, k * columns // outs : (k + 1) * columns // outs]

    extra = () if after is None else (after,)
    vmem, smem = pl.BlockSpec(memory_space=pltpu.VMEM), pl.BlockSpec(memory_space=pltpu.SMEM)
    return pl.pallas_call(
        kernel,
        in_specs=[smem, smem] + [pl.BlockSpec(memory_space=pl.ANY)] * (10 + len(extra)),
        out_specs=[vmem] * outs,
        out_shape=[jax.ShapeDtypeStruct((live, chunks * columns // outs), BF16)] * outs,
        scratch_shapes=[
            pltpu.VMEM((live, 256), BF16),
            pltpu.VMEM((256, chunks * columns), BF16),
            pltpu.SemaphoreType.DMA((chunks, 10)),
        ],
        compiler_params=pltpu.CompilerParams(vmem_limit_bytes=SPACE),
        cost_estimate=pl.CostEstimate(
            flops=2 * live * 256 * chunks * columns,
            bytes_accessed=2 * chunks * columns * (live + 256),
            transcendentals=0,
        ),
    )(index, lengths, *pieces, *extra)


TURNS = (0, 2, 1, 3)


def load_rows(index_ref, near, far, x_ref, sems):
    live = x_ref.shape[0] // 2

    @pl.when(pl.program_id(0) == 0)
    def _():
        copies = [pltpu.make_async_copy(near, x_ref.at[:live], sems.at[0])]
        quarter = lax.rem(index_ref[0], 4)
        for k, block in enumerate(far):
            piece = block.shape[1]
            at = ((quarter ^ TURNS[k % 4]) * (len(far) // 4) + k // 4) * piece
            cols = pl.ds(pl.multiple_of(at, piece), piece)
            copies.append(pltpu.make_async_copy(block, x_ref.at[live:, cols], sems.at[1 + k]))
        for copy in copies:
            copy.start()
        for copy in copies:
            copy.wait()


def add_share(steps, out_ref, x_ref, proj_ref):
    step = pl.program_id(0)
    shares = 4 if steps >= 4 else 2 if steps >= 2 else 1
    depth = x_ref.shape[1] // shares
    at = pl.ds(pl.multiple_of(lax.rem(step, shares) * depth, depth), depth)

    @pl.when(step < shares)
    def _():
        part = dot_nt(x_ref[:, at], proj_ref[:, at])
        out_ref[...] = jnp.where(step == 0, part, out_ref[...] + part)


def forward_kernel(pieces, steps, first, index_ref, *refs):
    blocks, refs = refs[:pieces], refs[pieces:]
    gate_w, up_w, proj_hid, *refs = refs
    if first:
        proj_in, silu_ref, grad_ref, hid_ref, in_ref, x_ref, sems = refs
    else:
        _, _, hid_prev, silu_ref, grad_ref, hid_ref, x_ref, sems = refs
    load_rows(index_ref, blocks[0], blocks[1:], x_ref, sems)
    if first:
        add_share(steps, in_ref, x_ref, proj_in)
    silu_val, silu_grad = silu_parts(dot(x_ref[...], gate_w[...]))
    up = dot(x_ref[...], up_w[...])
    silu_ref[...] = silu_val
    grad_ref[...] = up * silu_grad
    part = dot_nt((silu_val * up).astype(BF16), proj_hid[...])
    before = jnp.zeros_like(part) if first else hid_prev[...]
    hid_ref[...] = jnp.where(pl.program_id(0) == 0, before, hid_ref[...]) + part


def backward_kernel(pieces, steps, index_ref, *refs):
    blocks, refs = refs[:pieces], refs[pieces:]
    down_w, proj_cot, silu_ref, grad_ref, proj_gate, proj_up, *refs = refs
    gate_ref, up_ref, cot_ref, x_ref, sems = refs
    load_rows(index_ref, blocks[0], blocks[1:], x_ref, sems)
    add_share(steps, cot_ref, x_ref, proj_cot)
    dhidden = dot_nt(x_ref[...], down_w[...])
    up = dot_nt((dhidden * silu_ref[...]).astype(BF16), proj_up[...])
    gate = dot_nt((dhidden * grad_ref[...]).astype(BF16), proj_gate[...])
    first = pl.program_id(0) == 0
    up_ref[...] = jnp.where(first, up, up_ref[...] + up)
    gate_ref[...] = jnp.where(first, gate, gate_ref[...] + gate)


def rows_call(kernel, tiles, index, rows, width, blocks, specs, operands, outs, work, aliases):
    start, stop = tiles
    anywhere = pl.BlockSpec(memory_space=pl.ANY)
    kinds = {
        "wide": lambda shape: pl.BlockSpec((shape[0], TILE), lambda n, i: (0, start + n)),
        "down": lambda shape: pl.BlockSpec((width, TILE), lambda n, i: (0, start + n)),
        "across": lambda shape: pl.BlockSpec((TILE, width), lambda n, i: (start + n, 0)),
        "side": lambda shape: pl.BlockSpec((RANK, TILE), lambda n, i: (0, start + n)),
        "whole": lambda shape: pl.BlockSpec(shape, lambda n, i: (0, 0)),
        "any": lambda shape: anywhere,
    }
    return pl.pallas_call(
        kernel,
        grid_spec=pltpu.PrefetchScalarGridSpec(
            num_scalar_prefetch=1,
            grid=(stop - start,),
            in_specs=[anywhere] * len(blocks) + [kinds[s](x.shape) for s, x in zip(specs, operands)],
            out_specs=[kinds[s](o) for s, o in outs],
            scratch_shapes=[pltpu.VMEM((rows, width), BF16), pltpu.SemaphoreType.DMA((1 + len(blocks),))],
        ),
        out_shape=[jax.ShapeDtypeStruct(o, F32) for _, o in outs],
        input_output_aliases=aliases,
        compiler_params=pltpu.CompilerParams(vmem_limit_bytes=SPACE),
        cost_estimate=pl.CostEstimate(
            flops=2 * rows * width * (stop - start) * TILE * work,
            bytes_accessed=2 * width * (stop - start) * TILE * work,
            transcendentals=0,
        ),
    )(index, *blocks, *operands)


def forward_part(tiles, index, blocks, gate_weight, up_weight, proj_hidden, proj_input, prev):
    width, cols = gate_weight.shape
    rows = 2 * blocks[0].shape[0]
    first = prev is None
    specs = ["down", "down", "side"] + (["whole"] if first else ["any", "any", "whole"])
    operands = [gate_weight, up_weight, proj_hidden] + ([proj_input] if first else list(prev))
    outs = [("wide", (rows, cols))] * 2 + [("whole", (rows, RANK))] * (2 if first else 1)
    before = 1 + len(blocks) + 3
    aliases = {} if first else {before: 0, before + 1: 1}
    kernel = lambda *refs: forward_kernel(len(blocks), tiles[1] - tiles[0], first, *refs)
    return rows_call(kernel, tiles, index, rows, width, blocks, specs, operands, outs, 2, aliases)


def backward_part(index, near, far, down_weight, proj_cotangent, silu, grad, proj_gate, proj_up):
    cols, width = down_weight.shape
    rows = 2 * near.shape[0]
    specs = ["across", "whole"] + ["wide"] * 2 + ["side", "side"]
    operands = [down_weight, proj_cotangent, silu, grad, proj_gate, proj_up]
    kernel = lambda *refs: backward_kernel(1 + len(far), cols // TILE, *refs)
    return rows_call(kernel, (0, cols // TILE), index, rows, width, (near, *far), specs, operands,
                     [("whole", (rows, RANK))] * 3, 1, {})


MINE = 3 * RANK // 16


def sketch_kernel(index_ref, lengths_ref, gate_ref, up_ref, cot_ref, in_ref, hid_ref, keep_ref, give_ref, even_ref, odd_ref):
    live = gate_ref.shape[0] // 2
    far_first = index_ref[0] // 8
    scale = 1.0 / math.sqrt(LEN)
    at = lax.broadcasted_iota(jnp.int32, (live, 1), 0)
    for half in range(2):
        own, start = group_lengths(lengths_ref, half)
        rows = pl.ds(pl.multiple_of((far_first ^ half) * live, 16), live)
        outs = jnp.concatenate([gate_ref[rows], up_ref[rows], cot_ref[rows]], axis=1)
        ins = jnp.concatenate([in_ref[rows], hid_ref[rows]], axis=1)
        for k in range(SEQS // 2):
            s = half * (SEQS // 2) + k
            weight = jnp.where((at >= start[k]) & (at < start[k] + own[k]), scale, 0.0)
            got = lax.dot_general(
                outs * weight, ins, (((0,), (0,)), ((), ())),
                precision=HIGHEST, preferred_element_type=F32,
            )
            cols = slice(s * RANK, (s + 1) * RANK)
            got = jnp.concatenate([got[: 2 * RANK, :RANK], got[2 * RANK :, RANK:]], axis=0)
            for place in range(16):
                z, y, c = place // 4, (place // 2) % 2, place % 2
                at_row = (4 * y + z) * MINE
                rows_of = got[place * MINE : (place + 1) * MINE]
                (odd_ref if c else even_ref)[at_row : at_row + MINE, cols] = rows_of
    odd = lax.rem(index_ref[0], 2) == 1
    keep_ref[...] = jnp.where(odd, odd_ref[...], even_ref[...])
    give_ref[...] = jnp.where(odd, even_ref[...], odd_ref[...])


def packed_branch(live, index, lengths, tokens, cotangent, gate_weight, up_weight, down_weight,
                  proj_input, proj_cotangent, proj_hidden, proj_up, proj_gate, queries):
    z, y, c = index // 4, (index // 2) % 2, index % 2
    width = tokens.shape[1]
    half, piece = width // 2, width // 8
    index_ref = index.reshape(1)

    tok_z, tok_y = send(tokens, ZPAIR), send(tokens, YSWAP)
    tok_core = send(tokens, CORE)
    tok_dz, tok_dy = send(tok_y[:, :half], ZPAIR), send(tok_z[:, half:], YSWAP)
    tok_pieces = (tokens, tok_z, tok_y, tok_dz, tok_dy, tok_core) + tuple(
        send(x, CORE) for x in (tok_z, tok_y, tok_dz, tok_dy))
    first_0, first_1 = pack(index_ref, lengths, tok_pieces, live, True, outs=2)
    got_0, got_1 = send(first_0, ZFAR), send(first_1, ZFAR)
    cotangent, first_0 = tie(cotangent, first_0)
    cot_z, cot_y = send(cotangent, ZPAIR), send(cotangent, YSWAP)
    (tok_near,) = pack(index_ref, lengths, tok_pieces, live, False, after=first_0)
    low, high = cot_y[:, :half], cot_z[:, half:]
    low, high, got_0, tok_near = tie(low, high, got_0, tok_near)
    cot_dz, cot_dy = send(low, ZPAIR), send(high, YSWAP)
    far_0 = send(got_0, YSWAP)
    got_1, cot_dz, cot_dy, cotangent, cot_z, cot_y = tie(got_1, cot_dz, cot_dy, cotangent, cot_z, cot_y)
    far_1 = send(got_1, YSWAP)
    cot_pieces = (cotangent, cot_z, cot_y, cot_dz, cot_dy)
    cot_pieces += tuple(send(x, CORE) for x in cot_pieces)
    (first_2,) = pack(index_ref, lengths, cot_pieces, live, True, after=got_1)
    got_2 = send(first_2, ZFAR)
    far_1, first_2 = tie(far_1, first_2)

    def cross(got, from_y):
        return (got, from_y, send(got, CORE), send(from_y, CORE))

    tok_far = cross(got_0, far_0) + cross(got_1, far_1)
    turned = (proj_hidden.T, proj_input.T)
    tiles = gate_weight.shape[1] // TILE
    cut = -(-tiles // 2)
    forward = lambda part, prev: forward_part(
        part, index_ref, (tok_near, *tok_far), gate_weight, up_weight, *turned, prev)
    silu, grad, p_hid, a_in = forward((0, cut), None)
    (cot_near,) = pack(index_ref, lengths, cot_pieces, live, False, after=p_hid)
    queries, p_hid = tie(queries, p_hid)
    other = send(queries, ZPAIR)
    pair = jnp.where(z % 2 == 0, jnp.concatenate([queries, other], 1), jnp.concatenate([other, queries], 1))
    got_2, p_hid, cot_near, pair = tie(got_2, p_hid, cot_near, pair)
    far_2 = send(got_2, YSWAP)
    other = send(pair, ZFAR)
    all_queries = jnp.where(z // 2 == 0, jnp.concatenate([pair, other], 1), jnp.concatenate([other, pair], 1))
    silu, grad, p_hid = forward((cut, tiles), (silu, grad, p_hid))
    far_2, p_hid, all_queries = tie(far_2, p_hid, all_queries)
    cot_far = cross(got_2, far_2)
    p_gate, p_up, a_cot = backward_part(
        index_ref, cot_near, cot_far, down_weight, proj_cotangent.T, silu, grad, proj_gate.T, proj_up.T)

    vmem, smem = pl.BlockSpec(memory_space=pltpu.VMEM), pl.BlockSpec(memory_space=pltpu.SMEM)
    rows = 8 * MINE
    flat = jax.ShapeDtypeStruct((rows, SEQS * RANK), F32)
    keep, give = pl.pallas_call(
        sketch_kernel,
        in_specs=[smem] * 2 + [vmem] * 5,
        out_specs=[vmem] * 2,
        out_shape=[flat] * 2,
        scratch_shapes=[pltpu.VMEM(flat.shape, F32)] * 2,
        compiler_params=pltpu.CompilerParams(vmem_limit_bytes=SPACE),
    )(index_ref, lengths, p_gate, p_up, a_cot, a_in, p_hid)
    p = keep + send(give, CORE)
    low, high = p[: rows // 2], p[rows // 2 :]
    p = jnp.where(y == 0, low, high) + send(jnp.where(y == 0, high, low), YSWAP)
    p = p + send(p, ZPAIR)
    p = p + send(p, ZFAR)
    total = lax.dynamic_slice_in_dim(p, z * MINE, MINE, 0)
    logged = total.reshape(MINE, SEQS, RANK).transpose(1, 0, 2).reshape(SEQS, MINE * RANK)
    lines = p.reshape(4 * MINE, SEQS, RANK).transpose(1, 0, 2).reshape(SEQS, 4 * MINE * RANK)
    stats = jnp.dot(jnp.concatenate([lines, all_queries], axis=0), lines.T, precision=HIGHEST)
    stats = stats + send(stats, CORE)
    stats = stats + send(stats, YSWAP)
    scores = pl.pallas_call(
        solve_kernel, out_shape=jax.ShapeDtypeStruct((queries.shape[0], SEQS), F32)
    )(stats)
    return (logged, scores)


SIZES = (192, 224, 256)


def on_device_424(
    tokens,
    cotangent,
    lengths,
    gate_weight,
    up_weight,
    down_weight,
    proj_input,
    proj_cotangent,
    proj_hidden,
    proj_up,
    proj_gate,
    queries,
):
    index = lax.axis_index("dp")
    halves = lengths.reshape(2, SEQS // 2).sum(axis=1)
    most = jnp.maximum(halves[0], halves[1])
    operands = (index, lengths, tokens, cotangent, gate_weight, up_weight, down_weight, proj_input,
                proj_cotangent, proj_hidden, proj_up, proj_gate, queries)

    def at_least(sizes):
        branch = lambda *args: packed_branch(sizes[0], *args)
        if len(sizes) == 1:
            return branch
        return lambda *args: lax.cond(most <= sizes[0], branch, at_least(sizes[1:]), *args)

    return at_least(SIZES)(*operands)


def solution(mesh):
    placed = (
        P(("group", "dp"), None),
        P(("group", "dp"), None),
        P("group"),
        P(None, "dp"),
        P(None, "dp"),
        P("dp", None),
        P(),
        P(),
        P("dp", None),
        P("dp", None),
        P("dp", None),
        P("group", "dp"),
    )
    return jax.shard_map(
        on_device_424 if mesh.shape["dp"] == 16 else on_device,
        mesh=mesh,
        in_specs=placed,
        out_specs=(P("group", "dp"), P("group", None)),
        check_vma=False,
    )
```

```python
import math

import jax
import jax.numpy as jnp
from jax import lax
from jax.experimental import pallas as pl
from jax.experimental.pallas import tpu as pltpu
from jax.sharding import PartitionSpec as P

RANK = 64
LEN = 64
SEQS = 8
HIGHEST = lax.Precision.HIGHEST
F32 = jnp.float32
BF16 = jnp.bfloat16


def silu_parts(gate):
    sigma = jax.nn.sigmoid(gate)
    return (gate * sigma, sigma * (1.0 + gate * (1.0 - sigma)))


def block_sketch(weight_rows, out_proj, in_proj):
    out_blocks = out_proj.reshape(SEQS, LEN, RANK)
    in_blocks = in_proj.reshape(SEQS, LEN, RANK)
    sketch = jnp.einsum(
        "sl,slo,sli->soi", weight_rows, out_blocks, in_blocks, precision=HIGHEST
    )
    return sketch.reshape(SEQS, RANK * RANK)


def on_device(
    tokens,
    cotangent,
    lengths,
    gate_weight,
    up_weight,
    down_weight,
    proj_input,
    proj_cotangent,
    proj_hidden,
    proj_up,
    proj_gate,
    queries,
):
    scale = 1.0 / math.sqrt(LEN)
    piece = lax.all_gather(tokens, "dp", axis=0, tiled=True)
    gate = jnp.dot(piece, gate_weight, preferred_element_type=F32)
    up = jnp.dot(piece, up_weight, preferred_element_type=F32)
    input_all = jnp.dot(piece, proj_input, preferred_element_type=F32)
    silu_val, silu_grad = silu_parts(gate)
    hidden = (silu_val * up).astype(BF16)
    piece = lax.all_gather(cotangent, "dp", axis=0, tiled=True)
    dhidden = lax.dot_general(
        piece, down_weight, (((1,), (1,)), ((), ())), preferred_element_type=F32
    )
    cot_all = jnp.dot(piece, proj_cotangent, preferred_element_type=F32)
    d_up = (dhidden * silu_val).astype(BF16)
    d_gate = (dhidden * up * silu_grad).astype(BF16)
    p_hid = jnp.dot(hidden, proj_hidden, preferred_element_type=F32)
    p_up = jnp.dot(d_up, proj_up, preferred_element_type=F32)
    p_gate = jnp.dot(d_gate, proj_gate, preferred_element_type=F32)
    a_hid, a_up, a_gate = lax.psum((p_hid, p_up, p_gate), "dp")
    live = (lax.iota(jnp.int32, LEN)[None, :] < lengths[:, None]).astype(F32) * scale
    logged = jnp.concatenate(
        [
            block_sketch(live, a_gate, input_all),
            block_sketch(live, a_up, input_all),
            block_sketch(live, cot_all, a_hid),
        ],
        axis=1,
    )
    width = queries.shape[1]
    logged_part = lax.dynamic_slice_in_dim(logged, lax.axis_index("dp") * width, width, 1)
    full_queries = lax.all_gather(queries, "dp", axis=1, tiled=True)
    gram = jnp.dot(logged, logged.T, precision=HIGHEST)
    cross = jnp.dot(full_queries, logged.T, precision=HIGHEST)
    damping = jnp.trace(gram) / SEQS
    system = gram + damping * jnp.eye(SEQS, dtype=F32)
    factor = jnp.linalg.cholesky(system)
    solved = jax.scipy.linalg.cho_solve((factor, True), cross.T)
    scores = damping * solved.T
    return (logged_part, scores)


PLACES = [(z, y, c) for z in range(4) for y in range(2) for c in range(2)]


def spot(z, y, c):
    return 4 * z + 2 * y + c


CORE = [(spot(z, y, c), spot(z, y, 1 - c)) for z, y, c in PLACES]
YSWAP = [(spot(z, y, c), spot(z, 1 - y, c)) for z, y, c in PLACES]
ZPAIR = [(spot(z, y, c), spot(z ^ 1, y, c)) for z, y, c in PLACES]
ZFAR = [(spot(z, y, c), spot(z ^ 2, y, c)) for z, y, c in PLACES]


def send(x, pairs):
    return lax.ppermute(x, "dp", pairs)


def solve_kernel(stats_ref, out_ref):
    stats = stats_ref[...]
    gram = stats[:SEQS]
    row = lax.broadcasted_iota(jnp.int32, (SEQS, SEQS), 0)
    col = lax.broadcasted_iota(jnp.int32, (SEQS, SEQS), 1)
    eye = (row == col).astype(F32)
    damping = jnp.sum(gram * eye) / SEQS
    left = gram + damping * eye
    right = eye
    for k in range(SEQS):
        pivot = left[k : k + 1, k : k + 1]
        left_row = left[k : k + 1, :] / pivot
        right_row = right[k : k + 1, :] / pivot
        factor = jnp.where(row[:, :1] == k, 0.0, left[:, k : k + 1])
        left = jnp.where(row == k, left_row, left - factor * left_row)
        right = jnp.where(row == k, right_row, right - factor * right_row)
    cross = stats[SEQS:]
    out_ref[...] = damping * jnp.dot(cross, right, precision=HIGHEST, preferred_element_type=F32)


def tie(*arrays):
    return lax.optimization_barrier(arrays)


def dot(a, b):
    return jnp.dot(a, b, preferred_element_type=F32)


def dot_nt(a, b):
    return lax.dot_general(a, b, (((1,), (1,)), ((), ())), preferred_element_type=F32)


TILE = 256
SPACE = 32 * 2**20


def group_lengths(lengths_ref, half):
    own = [lengths_ref[half * (SEQS // 2) + s] for s in range(SEQS // 2)]
    start = [0]
    for length in own[:-1]:
        start.append(start[-1] + length)
    return own, start


def packed_places(index, lengths_ref):
    z, y, c = index // 4, (index // 2) % 2, index % 2
    own, start = group_lengths(lengths_ref, z // 2)
    row = lax.broadcasted_iota(jnp.int32, (1, 256), 1)
    seq = ((row // 32) % 2 ^ (z % 2)) * 2 + ((row // 64) % 2 ^ y)
    token = (row // 128 ^ c) * 32 + row % 32
    place = jnp.full((1, 256), -1, jnp.int32)
    for s in range(SEQS // 2):
        place = jnp.where((seq == s) & (token < own[s]), start[s] + token, place)
    return place


def pack(index, lengths, pieces, live, quarter_only, after=None, outs=1):
    width = pieces[0].shape[1]
    columns = width // 4
    chunks = 1 if quarter_only else 4

    def kernel(index_ref, lengths_ref, *refs):
        blocks, refs = refs[:10], refs[10 + (after is not None) :]
        out_refs, (pick_ref, rows_ref, sems) = refs[:outs], refs[outs:]

        def copy(chunk, k, source):
            rows = pl.ds(128 * (k // 5) + 32 * min(k % 5, 3), 32)
            cols = pl.ds(chunk * columns, columns)
            return pltpu.make_async_copy(source, rows_ref.at[rows, cols], sems.at[chunk, k])

        def part(block, at):
            if not isinstance(at, int):
                at = pl.multiple_of(at, columns)
            return block.at[:, pl.ds(at, columns)]

        for chunk in range(chunks):
            quarter = lax.rem(index_ref[0], 4) if quarter_only else chunk
            for k in (0, 1, 2, 5, 6, 7):
                copy(chunk, k, part(blocks[k], quarter * columns)).start()
            for k in (3, 8):
                if not quarter_only:
                    block = blocks[k + quarter // 2]
                    copy(chunk, k, part(block, quarter % 2 * columns)).start()
                else:
                    for side in range(2):

                        @pl.when(quarter // 2 == side)
                        def _():
                            at = lax.rem(quarter, 2) * columns
                            copy(chunk, k, part(blocks[k + side], at)).start()

        row = lax.broadcasted_iota(jnp.int32, (live, 256), 0)
        place = packed_places(index_ref[0], lengths_ref)
        pick_ref[...] = (row == place).astype(F32).astype(BF16)
        for chunk in range(chunks):
            for k in (0, 1, 2, 3, 5, 6, 7, 8):
                copy(chunk, k, part(blocks[k], 0)).wait()
            cols = slice(chunk * columns, (chunk + 1) * columns)
            got = dot(pick_ref[...], rows_ref[:, cols]).astype(BF16)
            if outs == 1:
                out_refs[0][:, cols] = got
            else:
                for k in range(outs):
                    out_refs[k][...] = got[:, k * columns // outs : (k + 1) * columns // outs]

    extra = () if after is None else (after,)
    vmem, smem = pl.BlockSpec(memory_space=pltpu.VMEM), pl.BlockSpec(memory_space=pltpu.SMEM)
    return pl.pallas_call(
        kernel,
        in_specs=[smem, smem] + [pl.BlockSpec(memory_space=pl.ANY)] * (10 + len(extra)),
        out_specs=[vmem] * outs,
        out_shape=[jax.ShapeDtypeStruct((live, chunks * columns // outs), BF16)] * outs,
        scratch_shapes=[
            pltpu.VMEM((live, 256), BF16),
            pltpu.VMEM((256, chunks * columns), BF16),
            pltpu.SemaphoreType.DMA((chunks, 10)),
        ],
        compiler_params=pltpu.CompilerParams(vmem_limit_bytes=SPACE),
        cost_estimate=pl.CostEstimate(
            flops=2 * live * 256 * chunks * columns,
            bytes_accessed=2 * chunks * columns * (live + 256),
            transcendentals=0,
        ),
    )(index, lengths, *pieces, *extra)


TURNS = (0, 2, 1, 3)


def load_rows(index_ref, near, far, x_ref, sems):
    live = x_ref.shape[0] // 2

    @pl.when(pl.program_id(0) == 0)
    def _():
        copies = [pltpu.make_async_copy(near, x_ref.at[:live], sems.at[0])]
        quarter = lax.rem(index_ref[0], 4)
        for k, block in enumerate(far):
            piece = block.shape[1]
            at = ((quarter ^ TURNS[k % 4]) * (len(far) // 4) + k // 4) * piece
            cols = pl.ds(pl.multiple_of(at, piece), piece)
            copies.append(pltpu.make_async_copy(block, x_ref.at[live:, cols], sems.at[1 + k]))
        for copy in copies:
            copy.start()
        for copy in copies:
            copy.wait()


def add_share(steps, out_ref, x_ref, proj_ref):
    step = pl.program_id(0)
    shares = 4 if steps >= 4 else 2 if steps >= 2 else 1
    depth = x_ref.shape[1] // shares
    at = pl.ds(pl.multiple_of(lax.rem(step, shares) * depth, depth), depth)

    @pl.when(step < shares)
    def _():
        part = dot_nt(x_ref[:, at], proj_ref[:, at])
        out_ref[...] = jnp.where(step == 0, part, out_ref[...] + part)


def forward_kernel(pieces, steps, first, index_ref, *refs):
    blocks, refs = refs[:pieces], refs[pieces:]
    gate_w, up_w, proj_hid, *refs = refs
    if first:
        proj_in, silu_ref, grad_ref, hid_ref, in_ref, x_ref, sems = refs
    else:
        _, _, hid_prev, silu_ref, grad_ref, hid_ref, x_ref, sems = refs
    load_rows(index_ref, blocks[0], blocks[1:], x_ref, sems)
    if first:
        add_share(steps, in_ref, x_ref, proj_in)
    silu_val, silu_grad = silu_parts(dot(x_ref[...], gate_w[...]))
    up = dot(x_ref[...], up_w[...])
    silu_ref[...] = silu_val
    grad_ref[...] = up * silu_grad
    part = dot_nt((silu_val * up).astype(BF16), proj_hid[...])
    before = jnp.zeros_like(part) if first else hid_prev[...]
    hid_ref[...] = jnp.where(pl.program_id(0) == 0, before, hid_ref[...]) + part


def backward_kernel(pieces, steps, index_ref, *refs):
    blocks, refs = refs[:pieces], refs[pieces:]
    down_w, proj_cot, silu_ref, grad_ref, proj_gate, proj_up, *refs = refs
    gate_ref, up_ref, cot_ref, x_ref, sems = refs
    load_rows(index_ref, blocks[0], blocks[1:], x_ref, sems)
    add_share(steps, cot_ref, x_ref, proj_cot)
    dhidden = dot_nt(x_ref[...], down_w[...])
    up = dot_nt((dhidden * silu_ref[...]).astype(BF16), proj_up[...])
    gate = dot_nt((dhidden * grad_ref[...]).astype(BF16), proj_gate[...])
    first = pl.program_id(0) == 0
    up_ref[...] = jnp.where(first, up, up_ref[...] + up)
    gate_ref[...] = jnp.where(first, gate, gate_ref[...] + gate)


def rows_call(kernel, tiles, index, rows, width, blocks, specs, operands, outs, work, aliases):
    start, stop = tiles
    anywhere = pl.BlockSpec(memory_space=pl.ANY)
    kinds = {
        "wide": lambda shape: pl.BlockSpec((shape[0], TILE), lambda n, i: (0, start + n)),
        "down": lambda shape: pl.BlockSpec((width, TILE), lambda n, i: (0, start + n)),
        "across": lambda shape: pl.BlockSpec((TILE, width), lambda n, i: (start + n, 0)),
        "side": lambda shape: pl.BlockSpec((RANK, TILE), lambda n, i: (0, start + n)),
        "whole": lambda shape: pl.BlockSpec(shape, lambda n, i: (0, 0)),
        "any": lambda shape: anywhere,
    }
    return pl.pallas_call(
        kernel,
        grid_spec=pltpu.PrefetchScalarGridSpec(
            num_scalar_prefetch=1,
            grid=(stop - start,),
            in_specs=[anywhere] * len(blocks) + [kinds[s](x.shape) for s, x in zip(specs, operands)],
            out_specs=[kinds[s](o) for s, o in outs],
            scratch_shapes=[pltpu.VMEM((rows, width), BF16), pltpu.SemaphoreType.DMA((1 + len(blocks),))],
        ),
        out_shape=[jax.ShapeDtypeStruct(o, F32) for _, o in outs],
        input_output_aliases=aliases,
        compiler_params=pltpu.CompilerParams(vmem_limit_bytes=SPACE),
        cost_estimate=pl.CostEstimate(
            flops=2 * rows * width * (stop - start) * TILE * work,
            bytes_accessed=2 * width * (stop - start) * TILE * work,
            transcendentals=0,
        ),
    )(index, *blocks, *operands)


def forward_part(tiles, index, blocks, gate_weight, up_weight, proj_hidden, proj_input, prev):
    width, cols = gate_weight.shape
    rows = 2 * blocks[0].shape[0]
    first = prev is None
    specs = ["down", "down", "side"] + (["whole"] if first else ["any", "any", "whole"])
    operands = [gate_weight, up_weight, proj_hidden] + ([proj_input] if first else list(prev))
    outs = [("wide", (rows, cols))] * 2 + [("whole", (rows, RANK))] * (2 if first else 1)
    before = 1 + len(blocks) + 3
    aliases = {} if first else {before: 0, before + 1: 1}
    kernel = lambda *refs: forward_kernel(len(blocks), tiles[1] - tiles[0], first, *refs)
    return rows_call(kernel, tiles, index, rows, width, blocks, specs, operands, outs, 2, aliases)


def backward_part(index, near, far, down_weight, proj_cotangent, silu, grad, proj_gate, proj_up):
    cols, width = down_weight.shape
    rows = 2 * near.shape[0]
    specs = ["across", "whole"] + ["wide"] * 2 + ["side", "side"]
    operands = [down_weight, proj_cotangent, silu, grad, proj_gate, proj_up]
    kernel = lambda *refs: backward_kernel(1 + len(far), cols // TILE, *refs)
    return rows_call(kernel, (0, cols // TILE), index, rows, width, (near, *far), specs, operands,
                     [("whole", (rows, RANK))] * 3, 1, {})


MINE = 3 * RANK // 16


def sketch_kernel(index_ref, lengths_ref, gate_ref, up_ref, cot_ref, in_ref, hid_ref, keep_ref, give_ref, even_ref, odd_ref):
    live = gate_ref.shape[0] // 2
    far_first = index_ref[0] // 8
    scale = 1.0 / math.sqrt(LEN)
    at = lax.broadcasted_iota(jnp.int32, (live, 1), 0)
    for half in range(2):
        own, start = group_lengths(lengths_ref, half)
        rows = pl.ds(pl.multiple_of((far_first ^ half) * live, 16), live)
        outs = jnp.concatenate([gate_ref[rows], up_ref[rows], cot_ref[rows]], axis=1)
        ins = jnp.concatenate([in_ref[rows], hid_ref[rows]], axis=1)
        for k in range(SEQS // 2):
            s = half * (SEQS // 2) + k
            weight = jnp.where((at >= start[k]) & (at < start[k] + own[k]), scale, 0.0)
            got = lax.dot_general(
                outs * weight, ins, (((0,), (0,)), ((), ())),
                precision=HIGHEST, preferred_element_type=F32,
            )
            cols = slice(s * RANK, (s + 1) * RANK)
            got = jnp.concatenate([got[: 2 * RANK, :RANK], got[2 * RANK :, RANK:]], axis=0)
            for place in range(16):
                z, y, c = place // 4, (place // 2) % 2, place % 2
                at_row = (4 * y + z) * MINE
                rows_of = got[place * MINE : (place + 1) * MINE]
                (odd_ref if c else even_ref)[at_row : at_row + MINE, cols] = rows_of
    odd = lax.rem(index_ref[0], 2) == 1
    keep_ref[...] = jnp.where(odd, odd_ref[...], even_ref[...])
    give_ref[...] = jnp.where(odd, even_ref[...], odd_ref[...])


def packed_branch(live, index, lengths, tokens, cotangent, gate_weight, up_weight, down_weight,
                  proj_input, proj_cotangent, proj_hidden, proj_up, proj_gate, queries):
    z, y, c = index // 4, (index // 2) % 2, index % 2
    width = tokens.shape[1]
    half, piece = width // 2, width // 8
    index_ref = index.reshape(1)

    tok_z, tok_y = send(tokens, ZPAIR), send(tokens, YSWAP)
    tok_core = send(tokens, CORE)
    tok_dz, tok_dy = send(tok_y[:, :half], ZPAIR), send(tok_z[:, half:], YSWAP)
    tok_pieces = (tokens, tok_z, tok_y, tok_dz, tok_dy, tok_core) + tuple(
        send(x, CORE) for x in (tok_z, tok_y, tok_dz, tok_dy))
    first_0, first_1 = pack(index_ref, lengths, tok_pieces, live, True, outs=2)
    got_0, got_1 = send(first_0, ZFAR), send(first_1, ZFAR)
    cotangent, first_0 = tie(cotangent, first_0)
    cot_z, cot_y = send(cotangent, ZPAIR), send(cotangent, YSWAP)
    (tok_near,) = pack(index_ref, lengths, tok_pieces, live, False, after=first_0)
    low, high = cot_y[:, :half], cot_z[:, half:]
    low, high, got_0, tok_near = tie(low, high, got_0, tok_near)
    cot_dz, cot_dy = send(low, ZPAIR), send(high, YSWAP)
    far_0 = send(got_0, YSWAP)
    got_1, cot_dz, cot_dy, cotangent, cot_z, cot_y = tie(got_1, cot_dz, cot_dy, cotangent, cot_z, cot_y)
    far_1 = send(got_1, YSWAP)
    cot_pieces = (cotangent, cot_z, cot_y, cot_dz, cot_dy)
    cot_pieces += tuple(send(x, CORE) for x in cot_pieces)
    (first_2,) = pack(index_ref, lengths, cot_pieces, live, True, after=got_1)
    got_2 = send(first_2, ZFAR)
    far_1, first_2 = tie(far_1, first_2)

    def cross(got, from_y):
        return (got, from_y, send(got, CORE), send(from_y, CORE))

    tok_far = cross(got_0, far_0) + cross(got_1, far_1)
    turned = (proj_hidden.T, proj_input.T)
    tiles = gate_weight.shape[1] // TILE
    cut = -(-tiles // 2)
    forward = lambda part, prev: forward_part(
        part, index_ref, (tok_near, *tok_far), gate_weight, up_weight, *turned, prev)
    silu, grad, p_hid, a_in = forward((0, cut), None)
    (cot_near,) = pack(index_ref, lengths, cot_pieces, live, False, after=p_hid)
    got_2, p_hid, cot_near, queries = tie(got_2, p_hid, cot_near, queries)
    far_2 = send(got_2, YSWAP)
    other = send(queries, ZPAIR)
    pair = jnp.where(z % 2 == 0, jnp.concatenate([queries, other], 1), jnp.concatenate([other, queries], 1))
    silu, grad, p_hid = forward((cut, tiles), (silu, grad, p_hid))
    far_2, p_hid, pair = tie(far_2, p_hid, pair)
    other = send(pair, ZFAR)
    cot_far = cross(got_2, far_2)
    p_gate, p_up, a_cot = backward_part(
        index_ref, cot_near, cot_far, down_weight, proj_cotangent.T, silu, grad, proj_gate.T, proj_up.T)

    p_gate, other = tie(p_gate, other)
    all_queries = jnp.where(z // 2 == 0, jnp.concatenate([pair, other], 1), jnp.concatenate([other, pair], 1))

    vmem, smem = pl.BlockSpec(memory_space=pltpu.VMEM), pl.BlockSpec(memory_space=pltpu.SMEM)
    rows = 8 * MINE
    flat = jax.ShapeDtypeStruct((rows, SEQS * RANK), F32)
    keep, give = pl.pallas_call(
        sketch_kernel,
        in_specs=[smem] * 2 + [vmem] * 5,
        out_specs=[vmem] * 2,
        out_shape=[flat] * 2,
        scratch_shapes=[pltpu.VMEM(flat.shape, F32)] * 2,
        compiler_params=pltpu.CompilerParams(vmem_limit_bytes=SPACE),
    )(index_ref, lengths, p_gate, p_up, a_cot, a_in, p_hid)
    p = keep + send(give, CORE)
    low, high = p[: rows // 2], p[rows // 2 :]
    p = jnp.where(y == 0, low, high) + send(jnp.where(y == 0, high, low), YSWAP)
    p = p + send(p, ZPAIR)
    p = p + send(p, ZFAR)
    total = lax.dynamic_slice_in_dim(p, z * MINE, MINE, 0)
    logged = total.reshape(MINE, SEQS, RANK).transpose(1, 0, 2).reshape(SEQS, MINE * RANK)
    lines = p.reshape(4 * MINE, SEQS, RANK).transpose(1, 0, 2).reshape(SEQS, 4 * MINE * RANK)
    stats = jnp.dot(jnp.concatenate([lines, all_queries], axis=0), lines.T, precision=HIGHEST)
    stats = stats + send(stats, CORE)
    stats = stats + send(stats, YSWAP)
    scores = pl.pallas_call(
        solve_kernel, out_shape=jax.ShapeDtypeStruct((queries.shape[0], SEQS), F32)
    )(stats)
    return (logged, scores)


SIZES = (192, 224, 256)


def on_device_424(
    tokens,
    cotangent,
    lengths,
    gate_weight,
    up_weight,
    down_weight,
    proj_input,
    proj_cotangent,
    proj_hidden,
    proj_up,
    proj_gate,
    queries,
):
    index = lax.axis_index("dp")
    first = lax.iota(jnp.int32, SEQS) < SEQS // 2
    most = jnp.maximum(jnp.sum(jnp.where(first, lengths, 0)), jnp.sum(jnp.where(first, 0, lengths)))
    operands = (index, lengths, tokens, cotangent, gate_weight, up_weight, down_weight, proj_input,
                proj_cotangent, proj_hidden, proj_up, proj_gate, queries)

    def at_least(sizes):
        branch = lambda *args: packed_branch(sizes[0], *args)
        if len(sizes) == 1:
            return branch
        return lambda *args: lax.cond(most > sizes[0], at_least(sizes[1:]), branch, *args)

    return at_least(SIZES)(*operands)


def solution(mesh):
    placed = (
        P(("group", "dp"), None),
        P(("group", "dp"), None),
        P("group"),
        P(None, "dp"),
        P(None, "dp"),
        P("dp", None),
        P(),
        P(),
        P("dp", None),
        P("dp", None),
        P("dp", None),
        P("group", "dp"),
    )
    return jax.shard_map(
        on_device_424 if mesh.shape["dp"] == 16 else on_device,
        mesh=mesh,
        in_specs=placed,
        out_specs=(P("group", "dp"), P("group", None)),
        check_vma=False,
    )
```

```python
import math

import jax
import jax.numpy as jnp
from jax import lax
from jax.experimental import pallas as pl
from jax.experimental.pallas import tpu as pltpu
from jax.sharding import PartitionSpec as P

RANK = 64
LEN = 64
SEQS = 8
HIGHEST = lax.Precision.HIGHEST
F32 = jnp.float32
BF16 = jnp.bfloat16


def silu_parts(gate):
    sigma = jax.nn.sigmoid(gate)
    return (gate * sigma, sigma * (1.0 + gate * (1.0 - sigma)))


def block_sketch(weight_rows, out_proj, in_proj):
    out_blocks = out_proj.reshape(SEQS, LEN, RANK)
    in_blocks = in_proj.reshape(SEQS, LEN, RANK)
    sketch = jnp.einsum(
        "sl,slo,sli->soi", weight_rows, out_blocks, in_blocks, precision=HIGHEST
    )
    return sketch.reshape(SEQS, RANK * RANK)


def on_device(
    tokens,
    cotangent,
    lengths,
    gate_weight,
    up_weight,
    down_weight,
    proj_input,
    proj_cotangent,
    proj_hidden,
    proj_up,
    proj_gate,
    queries,
):
    scale = 1.0 / math.sqrt(LEN)
    piece = lax.all_gather(tokens, "dp", axis=0, tiled=True)
    gate = jnp.dot(piece, gate_weight, preferred_element_type=F32)
    up = jnp.dot(piece, up_weight, preferred_element_type=F32)
    input_all = jnp.dot(piece, proj_input, preferred_element_type=F32)
    silu_val, silu_grad = silu_parts(gate)
    hidden = (silu_val * up).astype(BF16)
    piece = lax.all_gather(cotangent, "dp", axis=0, tiled=True)
    dhidden = lax.dot_general(
        piece, down_weight, (((1,), (1,)), ((), ())), preferred_element_type=F32
    )
    cot_all = jnp.dot(piece, proj_cotangent, preferred_element_type=F32)
    d_up = (dhidden * silu_val).astype(BF16)
    d_gate = (dhidden * up * silu_grad).astype(BF16)
    p_hid = jnp.dot(hidden, proj_hidden, preferred_element_type=F32)
    p_up = jnp.dot(d_up, proj_up, preferred_element_type=F32)
    p_gate = jnp.dot(d_gate, proj_gate, preferred_element_type=F32)
    a_hid, a_up, a_gate = lax.psum((p_hid, p_up, p_gate), "dp")
    live = (lax.iota(jnp.int32, LEN)[None, :] < lengths[:, None]).astype(F32) * scale
    logged = jnp.concatenate(
        [
            block_sketch(live, a_gate, input_all),
            block_sketch(live, a_up, input_all),
            block_sketch(live, cot_all, a_hid),
        ],
        axis=1,
    )
    width = queries.shape[1]
    logged_part = lax.dynamic_slice_in_dim(logged, lax.axis_index("dp") * width, width, 1)
    full_queries = lax.all_gather(queries, "dp", axis=1, tiled=True)
    gram = jnp.dot(logged, logged.T, precision=HIGHEST)
    cross = jnp.dot(full_queries, logged.T, precision=HIGHEST)
    damping = jnp.trace(gram) / SEQS
    system = gram + damping * jnp.eye(SEQS, dtype=F32)
    factor = jnp.linalg.cholesky(system)
    solved = jax.scipy.linalg.cho_solve((factor, True), cross.T)
    scores = damping * solved.T
    return (logged_part, scores)


PLACES = [(z, y, c) for z in range(4) for y in range(2) for c in range(2)]


def spot(z, y, c):
    return 4 * z + 2 * y + c


CORE = [(spot(z, y, c), spot(z, y, 1 - c)) for z, y, c in PLACES]
YSWAP = [(spot(z, y, c), spot(z, 1 - y, c)) for z, y, c in PLACES]
ZPAIR = [(spot(z, y, c), spot(z ^ 1, y, c)) for z, y, c in PLACES]
ZFAR = [(spot(z, y, c), spot(z ^ 2, y, c)) for z, y, c in PLACES]


def send(x, pairs):
    return lax.ppermute(x, "dp", pairs)


def solve_kernel(stats_ref, out_ref):
    stats = stats_ref[...]
    gram = stats[:SEQS]
    row = lax.broadcasted_iota(jnp.int32, (SEQS, SEQS), 0)
    col = lax.broadcasted_iota(jnp.int32, (SEQS, SEQS), 1)
    eye = (row == col).astype(F32)
    damping = jnp.sum(gram * eye) / SEQS
    left = gram + damping * eye
    right = eye
    for k in range(SEQS):
        pivot = left[k : k + 1, k : k + 1]
        left_row = left[k : k + 1, :] / pivot
        right_row = right[k : k + 1, :] / pivot
        factor = jnp.where(row[:, :1] == k, 0.0, left[:, k : k + 1])
        left = jnp.where(row == k, left_row, left - factor * left_row)
        right = jnp.where(row == k, right_row, right - factor * right_row)
    cross = stats[SEQS:]
    out_ref[...] = damping * jnp.dot(cross, right, precision=HIGHEST, preferred_element_type=F32)


def tie(*arrays):
    return lax.optimization_barrier(arrays)


def dot(a, b):
    return jnp.dot(a, b, preferred_element_type=F32)


def dot_nt(a, b):
    return lax.dot_general(a, b, (((1,), (1,)), ((), ())), preferred_element_type=F32)


TILE = 256
SPACE = 32 * 2**20


def group_lengths(lengths_ref, half):
    own = [lengths_ref[half * (SEQS // 2) + s] for s in range(SEQS // 2)]
    start = [0]
    for length in own[:-1]:
        start.append(start[-1] + length)
    return own, start


def packed_places(index, lengths_ref):
    z, y, c = index // 4, (index // 2) % 2, index % 2
    own, start = group_lengths(lengths_ref, z // 2)
    row = lax.broadcasted_iota(jnp.int32, (1, 256), 1)
    seq = ((row // 32) % 2 ^ (z % 2)) * 2 + ((row // 64) % 2 ^ y)
    token = (row // 128 ^ c) * 32 + row % 32
    place = jnp.full((1, 256), -1, jnp.int32)
    for s in range(SEQS // 2):
        place = jnp.where((seq == s) & (token < own[s]), start[s] + token, place)
    return place


def pack(index, lengths, pieces, live, quarter_only, after=None, outs=1):
    width = pieces[0].shape[1]
    columns = width // 4
    chunks = 1 if quarter_only else 4

    def kernel(index_ref, lengths_ref, *refs):
        blocks, refs = refs[:10], refs[10 + (after is not None) :]
        out_refs, (pick_ref, rows_ref, sems) = refs[:outs], refs[outs:]

        def copy(chunk, k, source):
            rows = pl.ds(128 * (k // 5) + 32 * min(k % 5, 3), 32)
            cols = pl.ds(chunk * columns, columns)
            return pltpu.make_async_copy(source, rows_ref.at[rows, cols], sems.at[chunk, k])

        def part(block, at):
            if not isinstance(at, int):
                at = pl.multiple_of(at, columns)
            return block.at[:, pl.ds(at, columns)]

        for chunk in range(chunks):
            quarter = lax.rem(index_ref[0], 4) if quarter_only else chunk
            for k in (0, 1, 2, 5, 6, 7):
                copy(chunk, k, part(blocks[k], quarter * columns)).start()
            for k in (3, 8):
                if not quarter_only:
                    block = blocks[k + quarter // 2]
                    copy(chunk, k, part(block, quarter % 2 * columns)).start()
                else:
                    for side in range(2):

                        @pl.when(quarter // 2 == side)
                        def _():
                            at = lax.rem(quarter, 2) * columns
                            copy(chunk, k, part(blocks[k + side], at)).start()

        row = lax.broadcasted_iota(jnp.int32, (live, 256), 0)
        place = packed_places(index_ref[0], lengths_ref)
        pick_ref[...] = (row == place).astype(F32).astype(BF16)
        for chunk in range(chunks):
            for k in (0, 1, 2, 3, 5, 6, 7, 8):
                copy(chunk, k, part(blocks[k], 0)).wait()
            cols = slice(chunk * columns, (chunk + 1) * columns)
            got = dot(pick_ref[...], rows_ref[:, cols]).astype(BF16)
            if outs == 1:
                out_refs[0][:, cols] = got
            else:
                for k in range(outs):
                    out_refs[k][...] = got[:, k * columns // outs : (k + 1) * columns // outs]

    extra = () if after is None else (after,)
    vmem, smem = pl.BlockSpec(memory_space=pltpu.VMEM), pl.BlockSpec(memory_space=pltpu.SMEM)
    return pl.pallas_call(
        kernel,
        in_specs=[smem, smem] + [pl.BlockSpec(memory_space=pl.ANY)] * (10 + len(extra)),
        out_specs=[vmem] * outs,
        out_shape=[jax.ShapeDtypeStruct((live, chunks * columns // outs), BF16)] * outs,
        scratch_shapes=[
            pltpu.VMEM((live, 256), BF16),
            pltpu.VMEM((256, chunks * columns), BF16),
            pltpu.SemaphoreType.DMA((chunks, 10)),
        ],
        compiler_params=pltpu.CompilerParams(vmem_limit_bytes=SPACE),
        cost_estimate=pl.CostEstimate(
            flops=2 * live * 256 * chunks * columns,
            bytes_accessed=2 * chunks * columns * (live + 256),
            transcendentals=0,
        ),
    )(index, lengths, *pieces, *extra)


TURNS = (0, 2, 1, 3)


def load_rows(index_ref, near, far, x_ref, sems):
    live = x_ref.shape[0] // 2

    @pl.when(pl.program_id(0) == 0)
    def _():
        copies = [pltpu.make_async_copy(near, x_ref.at[:live], sems.at[0])]
        quarter = lax.rem(index_ref[0], 4)
        for k, block in enumerate(far):
            piece = block.shape[1]
            at = ((quarter ^ TURNS[k % 4]) * (len(far) // 4) + k // 4) * piece
            cols = pl.ds(pl.multiple_of(at, piece), piece)
            copies.append(pltpu.make_async_copy(block, x_ref.at[live:, cols], sems.at[1 + k]))
        for copy in copies:
            copy.start()
        for copy in copies:
            copy.wait()


def add_share(steps, out_ref, x_ref, proj_ref):
    step = pl.program_id(0)
    shares = 4 if steps >= 4 else 2 if steps >= 2 else 1
    depth = x_ref.shape[1] // shares
    at = pl.ds(pl.multiple_of(lax.rem(step, shares) * depth, depth), depth)

    @pl.when(step < shares)
    def _():
        part = dot_nt(x_ref[:, at], proj_ref[:, at])
        out_ref[...] = jnp.where(step == 0, part, out_ref[...] + part)


def forward_kernel(pieces, steps, first, index_ref, *refs):
    blocks, refs = refs[:pieces], refs[pieces:]
    gate_w, up_w, proj_hid, *refs = refs
    if first:
        proj_in, silu_ref, grad_ref, hid_ref, in_ref, x_ref, sems = refs
    else:
        _, _, hid_prev, silu_ref, grad_ref, hid_ref, x_ref, sems = refs
    load_rows(index_ref, blocks[0], blocks[1:], x_ref, sems)
    if first:
        add_share(steps, in_ref, x_ref, proj_in)
    silu_val, silu_grad = silu_parts(dot(x_ref[...], gate_w[...]))
    up = dot(x_ref[...], up_w[...])
    silu_ref[...] = silu_val
    grad_ref[...] = up * silu_grad
    part = dot_nt((silu_val * up).astype(BF16), proj_hid[...])
    before = jnp.zeros_like(part) if first else hid_prev[...]
    hid_ref[...] = jnp.where(pl.program_id(0) == 0, before, hid_ref[...]) + part


def backward_kernel(pieces, steps, index_ref, *refs):
    blocks, refs = refs[:pieces], refs[pieces:]
    down_w, proj_cot, silu_ref, grad_ref, proj_gate, proj_up, *refs = refs
    gate_ref, up_ref, cot_ref, x_ref, sems = refs
    load_rows(index_ref, blocks[0], blocks[1:], x_ref, sems)
    add_share(steps, cot_ref, x_ref, proj_cot)
    dhidden = dot_nt(x_ref[...], down_w[...])
    up = dot_nt((dhidden * silu_ref[...]).astype(BF16), proj_up[...])
    gate = dot_nt((dhidden * grad_ref[...]).astype(BF16), proj_gate[...])
    first = pl.program_id(0) == 0
    up_ref[...] = jnp.where(first, up, up_ref[...] + up)
    gate_ref[...] = jnp.where(first, gate, gate_ref[...] + gate)


def rows_call(kernel, tiles, index, rows, width, blocks, specs, operands, outs, work, aliases):
    start, stop = tiles
    anywhere = pl.BlockSpec(memory_space=pl.ANY)
    kinds = {
        "wide": lambda shape: pl.BlockSpec((shape[0], TILE), lambda n, i: (0, start + n)),
        "down": lambda shape: pl.BlockSpec((width, TILE), lambda n, i: (0, start + n)),
        "across": lambda shape: pl.BlockSpec((TILE, width), lambda n, i: (start + n, 0)),
        "side": lambda shape: pl.BlockSpec((RANK, TILE), lambda n, i: (0, start + n)),
        "whole": lambda shape: pl.BlockSpec(shape, lambda n, i: (0, 0)),
        "any": lambda shape: anywhere,
    }
    return pl.pallas_call(
        kernel,
        grid_spec=pltpu.PrefetchScalarGridSpec(
            num_scalar_prefetch=1,
            grid=(stop - start,),
            in_specs=[anywhere] * len(blocks) + [kinds[s](x.shape) for s, x in zip(specs, operands)],
            out_specs=[kinds[s](o) for s, o in outs],
            scratch_shapes=[pltpu.VMEM((rows, width), BF16), pltpu.SemaphoreType.DMA((1 + len(blocks),))],
        ),
        out_shape=[jax.ShapeDtypeStruct(o, F32) for _, o in outs],
        input_output_aliases=aliases,
        compiler_params=pltpu.CompilerParams(vmem_limit_bytes=SPACE),
        cost_estimate=pl.CostEstimate(
            flops=2 * rows * width * (stop - start) * TILE * work,
            bytes_accessed=2 * width * (stop - start) * TILE * work,
            transcendentals=0,
        ),
    )(index, *blocks, *operands)


def forward_part(tiles, index, blocks, gate_weight, up_weight, proj_hidden, proj_input, prev):
    width, cols = gate_weight.shape
    rows = 2 * blocks[0].shape[0]
    first = prev is None
    specs = ["down", "down", "side"] + (["whole"] if first else ["any", "any", "whole"])
    operands = [gate_weight, up_weight, proj_hidden] + ([proj_input] if first else list(prev))
    outs = [("wide", (rows, cols))] * 2 + [("whole", (rows, RANK))] * (2 if first else 1)
    before = 1 + len(blocks) + 3
    aliases = {} if first else {before: 0, before + 1: 1}
    kernel = lambda *refs: forward_kernel(len(blocks), tiles[1] - tiles[0], first, *refs)
    return rows_call(kernel, tiles, index, rows, width, blocks, specs, operands, outs, 2, aliases)


def backward_part(index, near, far, down_weight, proj_cotangent, silu, grad, proj_gate, proj_up):
    cols, width = down_weight.shape
    rows = 2 * near.shape[0]
    specs = ["across", "whole"] + ["wide"] * 2 + ["side", "side"]
    operands = [down_weight, proj_cotangent, silu, grad, proj_gate, proj_up]
    kernel = lambda *refs: backward_kernel(1 + len(far), cols // TILE, *refs)
    return rows_call(kernel, (0, cols // TILE), index, rows, width, (near, *far), specs, operands,
                     [("whole", (rows, RANK))] * 3, 1, {})


MINE = 3 * RANK // 16


def sketch_kernel(index_ref, lengths_ref, gate_ref, up_ref, cot_ref, in_ref, hid_ref, keep_ref, give_ref, even_ref, odd_ref):
    live = gate_ref.shape[0] // 2
    far_first = index_ref[0] // 8
    scale = 1.0 / math.sqrt(LEN)
    at = lax.broadcasted_iota(jnp.int32, (live, 1), 0)
    for half in range(2):
        own, start = group_lengths(lengths_ref, half)
        rows = pl.ds(pl.multiple_of((far_first ^ half) * live, 16), live)
        outs = jnp.concatenate([gate_ref[rows], up_ref[rows], cot_ref[rows]], axis=1)
        ins = jnp.concatenate([in_ref[rows], hid_ref[rows]], axis=1)
        for k in range(SEQS // 2):
            s = half * (SEQS // 2) + k
            weight = jnp.where((at >= start[k]) & (at < start[k] + own[k]), scale, 0.0)
            got = lax.dot_general(
                outs * weight, ins, (((0,), (0,)), ((), ())),
                precision=HIGHEST, preferred_element_type=F32,
            )
            cols = slice(s * RANK, (s + 1) * RANK)
            got = jnp.concatenate([got[: 2 * RANK, :RANK], got[2 * RANK :, RANK:]], axis=0)
            for place in range(16):
                z, y, c = place // 4, (place // 2) % 2, place % 2
                at_row = (4 * y + z) * MINE
                rows_of = got[place * MINE : (place + 1) * MINE]
                (odd_ref if c else even_ref)[at_row : at_row + MINE, cols] = rows_of
    odd = lax.rem(index_ref[0], 2) == 1
    keep_ref[...] = jnp.where(odd, odd_ref[...], even_ref[...])
    give_ref[...] = jnp.where(odd, even_ref[...], odd_ref[...])


def packed_branch(live, index, lengths, tokens, cotangent, gate_weight, up_weight, down_weight,
                  proj_input, proj_cotangent, proj_hidden, proj_up, proj_gate, queries):
    z, y, c = index // 4, (index // 2) % 2, index % 2
    width = tokens.shape[1]
    half, piece = width // 2, width // 8
    index_ref = index.reshape(1)

    tok_z, tok_y = send(tokens, ZPAIR), send(tokens, YSWAP)
    tok_core = send(tokens, CORE)
    tok_dz, tok_dy = send(tok_y[:, :half], ZPAIR), send(tok_z[:, half:], YSWAP)
    tok_pieces = (tokens, tok_z, tok_y, tok_dz, tok_dy, tok_core) + tuple(
        send(x, CORE) for x in (tok_z, tok_y, tok_dz, tok_dy))
    first_0, first_1 = pack(index_ref, lengths, tok_pieces, live, True, outs=2)
    got_0, got_1 = send(first_0, ZFAR), send(first_1, ZFAR)
    cotangent, first_0 = tie(cotangent, first_0)
    cot_z, cot_y = send(cotangent, ZPAIR), send(cotangent, YSWAP)
    (tok_near,) = pack(index_ref, lengths, tok_pieces, live, False, after=first_0)
    low, high = cot_y[:, :half], cot_z[:, half:]
    low, high, got_0, tok_near = tie(low, high, got_0, tok_near)
    cot_dz, cot_dy = send(low, ZPAIR), send(high, YSWAP)
    far_0 = send(got_0, YSWAP)
    got_1, cot_dz, cot_dy, cotangent, cot_z, cot_y = tie(got_1, cot_dz, cot_dy, cotangent, cot_z, cot_y)
    far_1 = send(got_1, YSWAP)
    cot_pieces = (cotangent, cot_z, cot_y, cot_dz, cot_dy)
    cot_pieces += tuple(send(x, CORE) for x in cot_pieces)
    (first_2,) = pack(index_ref, lengths, cot_pieces, live, True, after=got_1)
    got_2 = send(first_2, ZFAR)
    far_1, first_2 = tie(far_1, first_2)

    def cross(got, from_y):
        return (got, from_y, send(got, CORE), send(from_y, CORE))

    tok_far = cross(got_0, far_0) + cross(got_1, far_1)
    turned = (proj_hidden.T, proj_input.T)
    tiles = gate_weight.shape[1] // TILE
    cut = -(-tiles // 2)
    forward = lambda part, prev: forward_part(
        part, index_ref, (tok_near, *tok_far), gate_weight, up_weight, *turned, prev)
    silu, grad, p_hid, a_in = forward((0, cut), None)
    (cot_near,) = pack(index_ref, lengths, cot_pieces, live, False, after=p_hid)
    got_2, p_hid, cot_near, queries = tie(got_2, p_hid, cot_near, queries)
    far_2 = send(got_2, YSWAP)
    other = send(queries, ZPAIR)
    pair = jnp.where(z % 2 == 0, jnp.concatenate([queries, other], 1), jnp.concatenate([other, queries], 1))
    silu, grad, p_hid = forward((cut, tiles), (silu, grad, p_hid))
    far_2, p_hid, pair = tie(far_2, p_hid, pair)
    other = send(pair, ZFAR)
    cot_far = cross(got_2, far_2)
    p_gate, p_up, a_cot = backward_part(
        index_ref, cot_near, cot_far, down_weight, proj_cotangent.T, silu, grad, proj_gate.T, proj_up.T)

    p_gate, other = tie(p_gate, other)
    all_queries = jnp.where(z // 2 == 0, jnp.concatenate([pair, other], 1), jnp.concatenate([other, pair], 1))

    vmem, smem = pl.BlockSpec(memory_space=pltpu.VMEM), pl.BlockSpec(memory_space=pltpu.SMEM)
    rows = 8 * MINE
    flat = jax.ShapeDtypeStruct((rows, SEQS * RANK), F32)
    keep, give = pl.pallas_call(
        sketch_kernel,
        in_specs=[smem] * 2 + [vmem] * 5,
        out_specs=[vmem] * 2,
        out_shape=[flat] * 2,
        scratch_shapes=[pltpu.VMEM(flat.shape, F32)] * 2,
        compiler_params=pltpu.CompilerParams(vmem_limit_bytes=SPACE),
    )(index_ref, lengths, p_gate, p_up, a_cot, a_in, p_hid)
    p = keep + send(give, CORE)
    low, high = p[: rows // 2], p[rows // 2 :]
    p = jnp.where(y == 0, low, high) + send(jnp.where(y == 0, high, low), YSWAP)
    p = p + send(p, ZPAIR)
    p = p + send(p, ZFAR)
    total = lax.dynamic_slice_in_dim(p, z * MINE, MINE, 0)
    logged = total.reshape(MINE, SEQS, RANK).transpose(1, 0, 2).reshape(SEQS, MINE * RANK)
    lines = p.reshape(4 * MINE, SEQS, RANK).transpose(1, 0, 2).reshape(SEQS, 4 * MINE * RANK)
    stats = jnp.dot(jnp.concatenate([lines, all_queries], axis=0), lines.T, precision=HIGHEST)
    stats = stats + send(stats, CORE)
    stats = stats + send(stats, YSWAP)
    scores = pl.pallas_call(
        solve_kernel, out_shape=jax.ShapeDtypeStruct((queries.shape[0], SEQS), F32)
    )(stats)
    return (logged, scores)


SIZES = (192, 208, 224, 256)


def on_device_424(
    tokens,
    cotangent,
    lengths,
    gate_weight,
    up_weight,
    down_weight,
    proj_input,
    proj_cotangent,
    proj_hidden,
    proj_up,
    proj_gate,
    queries,
):
    index = lax.axis_index("dp")
    first = lax.iota(jnp.int32, SEQS) < SEQS // 2
    most = jnp.maximum(jnp.sum(jnp.where(first, lengths, 0)), jnp.sum(jnp.where(first, 0, lengths)))
    operands = (index, lengths, tokens, cotangent, gate_weight, up_weight, down_weight, proj_input,
                proj_cotangent, proj_hidden, proj_up, proj_gate, queries)

    def at_least(sizes):
        branch = lambda *args: packed_branch(sizes[0], *args)
        if len(sizes) == 1:
            return branch
        return lambda *args: lax.cond(most > sizes[0], at_least(sizes[1:]), branch, *args)

    return at_least(SIZES)(*operands)


def solution(mesh):
    placed = (
        P(("group", "dp"), None),
        P(("group", "dp"), None),
        P("group"),
        P(None, "dp"),
        P(None, "dp"),
        P("dp", None),
        P(),
        P(),
        P("dp", None),
        P("dp", None),
        P("dp", None),
        P("group", "dp"),
    )
    return jax.shard_map(
        on_device_424 if mesh.shape["dp"] == 16 else on_device,
        mesh=mesh,
        in_specs=placed,
        out_specs=(P("group", "dp"), P("group", None)),
        check_vma=False,
    )
```
